32 devices in a mesh: grp: 2 (over x), tm: 8 (over z, y), row: 2 (over core).
Axes of the slice: x: 2, y: 2, z: 4, core: 2. Of those that a mesh axis runs over, the one named last changes fastest.
Arguments:
- frames: bfloat16 [16, 256, 64, 48], P(('grp', 'tm'), None, 'row'), parts along dimension 0, may hold values from 0 to 31, as said below
- clip_start: int32 [16], P('grp'), parts along dimension 0, may hold values 0 or 1
- semantic: int32 [16, 64, 48], P(('grp', 'tm'), 'row'), parts along dimension 0, may hold values from 0 to 18
- instance: int32 [16, 64, 48], P(('grp', 'tm'), 'row'), parts along dimension 0, may hold values from 0 to 63
- aspp_point: bfloat16 [256, 512], replicated, may hold values from -0.25 to 0.25
- aspp_dilated: bfloat16 [3, 9, 256, 512], replicated, may hold values from -0.09375 to 0.09375
- pool_weight: bfloat16 [256, 512], replicated, may hold values from -0.25 to 0.25
- proj_weight: bfloat16 [256, 1280], replicated, may hold values from -0.15625 to 0.15625
- head_weight: bfloat16 [25, 96, 256], replicated, may hold values from -0.078125 to 0.078125
- out_weight: bfloat16 [4, 32], replicated, may hold values from -1 to 1
Outputs:
- predictions: float32 [16, 4, 64, 48], P(('grp', 'tm'), None, 'row'), parts along dimension 0
- losses: float32 [4], P('grp'), parts along dimension 0
The draws below stay inside these ranges and needn't reach their ends.
There are 2 independent parts, one for each index of `grp`. The reference program is written for one: setup_inputs(seed, part) draws one part's arguments, and reference() takes and returns one part's arrays. A program takes and returns all parts, laid end to end along the dimension named above; an argument that names none is the same for every part. Nothing has to cross between parts.
Inputs may be any that keep to these rules, and one draw needn't show every extreme that they name: `frames`: every entry is zero or positive.
All inputs are finite; a program needn't handle non-finite values.
Results may differ from the reference program's by a relative error of at most 0.0075.
Values may be sent and summed in bfloat16 or wider, within the bound.
A program may use at most 128 MiB of HBM per device.

```python
import jax
import jax.numpy as jnp
from jax import lax

CHANNELS = 256
ASPP = 256
HEAD = 32
CLASSES = 19
THING_FIRST = 11
INSTANCES = 64
W = 48
FRAMES = 8
HEIGHT = 64


def draw_frames(key, part):
    keys = jax.random.split(key, 2)
    shape = (FRAMES, CHANNELS, HEIGHT, W)
    channel_scale = jnp.exp(jax.random.uniform(keys[0], (1, CHANNELS, 1, 1), jnp.float32, jnp.log(0.3), jnp.log(3.0)))
    frame_pos = jnp.arange(FRAMES, dtype=jnp.float32).reshape(FRAMES, 1, 1, 1) / max(FRAMES - 1, 1)
    row_pos = jnp.arange(HEIGHT, dtype=jnp.float32).reshape(1, 1, HEIGHT, 1) / max(HEIGHT - 1, 1)
    scaling = channel_scale * (0.6 + 1.2 * frame_pos) * (0.6 + 0.8 * row_pos)
    values = jnp.minimum(jnp.abs(jax.random.normal(keys[1], shape, jnp.float32)), 4.0)
    return (values * scaling).astype(jnp.bfloat16)


def set_ends(drawn, rng, smallest, top_value):
    extent = drawn.shape
    spot = [jax.random.randint(jax.random.fold_in(rng, axis), (), 0, extent[axis]) for axis in range(len(extent))]
    drawn = drawn.at[tuple(spot)].set(smallest)
    longest = extent.index(max(extent))
    spot[longest] = (spot[longest] + 1) % extent[longest]
    return drawn.at[tuple(spot)].set(top_value)


def normal_values(stream_key, extent, scale, reach, kind=jnp.bfloat16):
    result = scale * jax.random.normal(stream_key, extent, jnp.float32)
    return jnp.clip(result, min=-reach, max=reach).astype(kind)


def setup_inputs(seed: int = 0, part: int = 0) -> dict:
    streams_of = jax.random.split(jax.random.key(seed), 11)
    part_splits = jax.random.split(jax.random.fold_in(streams_of[10], part), 11)
    frames = draw_frames(jax.random.fold_in(jax.random.fold_in(streams_of[10], part), 71), part)
    clip_start = set_ends((jax.random.randint(part_splits[1], (FRAMES,), 0, 6) < 1).astype(jnp.int32), jax.random.fold_in(part_splits[1], 1), 0, 1)
    semantic = set_ends(jax.random.randint(part_splits[2], (FRAMES, HEIGHT, W), 0, CLASSES), jax.random.fold_in(part_splits[2], 1), 0, CLASSES - 1).astype(jnp.int32)
    instance = set_ends(jax.random.randint(part_splits[3], (FRAMES, HEIGHT, W), 0, INSTANCES), jax.random.fold_in(part_splits[3], 1), 0, INSTANCES - 1).astype(jnp.int32)
    aspp_point = normal_values(streams_of[4], (ASPP, 2 * CHANNELS), (2 * CHANNELS) ** -0.5, 0.25)
    aspp_dilated = normal_values(streams_of[5], (3, 9, ASPP, 2 * CHANNELS), (18 * CHANNELS) ** -0.5, 0.09375)
    pool_weight = normal_values(streams_of[6], (ASPP, 2 * CHANNELS), (2 * CHANNELS) ** -0.5, 0.25)
    proj_weight = normal_values(streams_of[7], (ASPP, 5 * ASPP), (5 * ASPP) ** -0.5, 0.15625)
    head_weight = normal_values(streams_of[8], (25, 3 * HEAD, ASPP), (25 * ASPP) ** -0.5, 0.078125)
    out_weight = normal_values(streams_of[9], (4, HEAD), HEAD ** -0.5, 1.0)
    return {"frames": frames, "clip_start": clip_start, "semantic": semantic, "instance": instance, "aspp_point": aspp_point, "aspp_dilated": aspp_dilated, "pool_weight": pool_weight, "proj_weight": proj_weight, "head_weight": head_weight, "out_weight": out_weight}


DILATIONS = (6, 12, 18)
aspp_reach = 18
center_sigma = 8.0
offset_weight = 0.01


def conv_taps(padded, filters, margin, spread, kernel, row_count, col_count):
    running = None
    middle = kernel // 2
    for vertical in range(kernel):
        for lateral in range(kernel):
            row_top = margin + (vertical - middle) * spread
            col_left = margin + (lateral - middle) * spread
            window = padded[:, row_top:row_top + row_count, col_left:col_left + col_count]
            flattened = window.reshape(window.shape[0], row_count * col_count)
            partial_value = jnp.dot(filters[kernel * vertical + lateral], flattened, preferred_element_type=jnp.float32)
            running = partial_value if running is None else running + partial_value
    return running.reshape(-1, row_count, col_count)


def relu_bf16(values):
    return jnp.maximum(values, 0.0).astype(jnp.bfloat16)


def emit_heads(head_out, out_weight):
    groups = head_out.astype(jnp.float32).reshape(3, -1, head_out.shape[1], head_out.shape[2])
    weights32 = out_weight.astype(jnp.float32)
    center_map = jnp.einsum("c,crw->rw", weights32[0], groups[0])
    offset_map = jnp.einsum("oc,crw->orw", weights32[1:3], groups[1])
    depth_map = jnp.einsum("c,crw->rw", weights32[3], groups[2])
    return jnp.concatenate([center_map[None], offset_map, depth_map[None]], 0)


def reference(frames, clip_start, semantic, instance, aspp_point, aspp_dilated, pool_weight, proj_weight, head_weight, out_weight):
    ahead_index = ((jnp.arange(FRAMES, dtype=jnp.int32) + 1) % FRAMES).astype(jnp.int32)
    at_end = clip_start[ahead_index] == 1
    later = jnp.where(at_end[:, None, None, None], frames, frames[ahead_index])

    def frame_heads(paired):
        own_frame, later_frame = paired
        joined = jnp.concatenate([own_frame, later_frame], 0)
        channel_count = joined.shape[0]
        padded = jnp.pad(joined, ((0, 0), (aspp_reach, aspp_reach), (aspp_reach, aspp_reach)))
        flattened = joined.reshape(channel_count, HEIGHT * W)
        branches = [relu_bf16(jnp.dot(aspp_point, flattened, preferred_element_type=jnp.float32)).reshape(ASPP, HEIGHT, W)]
        for branch_index, spread in enumerate(DILATIONS):
            branches.append(relu_bf16(conv_taps(padded, aspp_dilated[branch_index], aspp_reach, spread, 3, HEIGHT, W)))
        pooled = (jnp.sum(joined, axis=(1, 2), dtype=jnp.float32) / (HEIGHT * W)).astype(jnp.bfloat16)
        pool_feature = relu_bf16(jnp.dot(pool_weight, pooled, preferred_element_type=jnp.float32))
        stacked = jnp.concatenate(branches, 0).reshape(4 * ASPP, HEIGHT * W)
        mixed = jnp.dot(proj_weight[:, :4 * ASPP], stacked, preferred_element_type=jnp.float32)
        mixed = mixed + jnp.dot(proj_weight[:, 4 * ASPP:], pool_feature, preferred_element_type=jnp.float32)[:, None]
        projected = relu_bf16(mixed).reshape(ASPP, HEIGHT, W)
        head_in = jnp.pad(projected, ((0, 0), (2, 2), (2, 2)))
        head_out = relu_bf16(conv_taps(head_in, head_weight, 2, 1, 5, HEIGHT, W))
        return emit_heads(head_out, out_weight)

    predictions = lax.map(frame_heads, (frames, later))

    counted = (semantic >= THING_FIRST) & (instance > 0)
    labels = jnp.arange(INSTANCES, dtype=jnp.int32)
    onehot = ((instance[:, None] == labels[None, :, None, None]) & counted[:, None]).astype(jnp.float32)
    row_pos = jnp.arange(HEIGHT, dtype=jnp.float32)[:, None] * jnp.ones((1, W), jnp.float32)
    col_pos = jnp.arange(W, dtype=jnp.float32)[None, :] * jnp.ones((HEIGHT, 1), jnp.float32)
    inst_stats = jnp.stack([jnp.sum(onehot, axis=(2, 3)), jnp.sum(onehot * row_pos, axis=(2, 3)), jnp.sum(onehot * col_pos, axis=(2, 3))], 1)
    pixel = jnp.einsum("fsk,fkhw->fshw", inst_stats, onehot, precision=lax.Precision.HIGHEST)
    counts = jnp.where(counted, pixel[:, 0], 1.0)
    centre_row = pixel[:, 1] / counts
    centre_col = pixel[:, 2] / counts
    distance = (row_pos - centre_row) * (row_pos - centre_row) + (col_pos - centre_col) * (col_pos - centre_col)
    heat = jnp.where(counted, jnp.exp(-distance / (2.0 * center_sigma * center_sigma)), 0.0)
    center_err = jnp.sum(jnp.square(predictions[:, 0] - heat))
    offset_err = jnp.sum(jnp.where(counted, jnp.abs(predictions[:, 1] - (centre_row - row_pos)) + jnp.abs(predictions[:, 2] - (centre_col - col_pos)), 0.0))
    counted_total = jnp.sum(counted.astype(jnp.float32))
    losses = jnp.stack([center_err / (FRAMES * HEIGHT * W), offset_weight * offset_err / jnp.maximum(counted_total, 1.0)])
    return predictions, losses
```

```python
import functools

import jax
import jax.numpy as jnp
import numpy as np
from jax import lax
from jax.experimental import pallas as pl
from jax.experimental.pallas import tpu as pltpu
from jax.sharding import PartitionSpec as P

THING_FIRST = 11
DILATIONS = (6, 12, 18)
REACH = 18
HEAD_REACH = 2
LANES = 128
center_sigma = 8.0
offset_weight = 0.01
MESH = pl.DeviceIdType.MESH


def dot_nt(a, b):
    return lax.dot_general(a, b, (((1,), (1,)), ((), ())), preferred_element_type=jnp.float32)


def dot_nn(a, b):
    return lax.dot_general(a, b, (((1,), (0,)), ((), ())), preferred_element_type=jnp.float32)


def kernel(
    frame_count,
    rows,
    cols,
    tile_rows,
    x_ref,
    flag_ref,
    label_ref,
    place_ref,
    point_hbm,
    dilated_hbm,
    pool_hbm,
    proj_hbm,
    head_hbm,
    out_w_ref,
    pred_ref,
    sums_ref,
    own,
    nxt,
    acc,
    point_w,
    dilated_w,
    pool_w,
    proj_w,
    head_w,
    projected,
    aux,
    small,
    small_in,
    total,
    total_in,
    local_sem,
    send_sem,
    recv_sem,
):
    g = lax.axis_index("grp")
    t = lax.axis_index("tm")
    r = lax.axis_index("row")
    prev = lax.rem(t + frame_count - 1, frame_count)
    later = lax.rem(t + 1, frame_count)
    sister = 1 - r
    cells = rows * cols
    tile = tile_rows * cols
    tiles = rows // tile_rows
    first = REACH * cols
    channels = x_ref.shape[1]
    rim = REACH * cols
    rest = cells - rim

    def local(index, src, dst):
        return pltpu.make_async_copy(src, dst, local_sem.at[index])

    copies = [
        local(0, x_ref, own.at[pl.ds(first, cells)]),
        local(1, dilated_hbm, dilated_w),
        local(2, point_hbm, point_w),
        local(3, pool_hbm, pool_w),
        local(4, proj_hbm, proj_w),
        local(5, head_hbm, head_w.at[:, pl.ds(0, head_hbm.shape[1])]),
    ]
    for copy in copies:
        copy.start()

    barrier = pltpu.get_barrier_semaphore()
    for other in ((g, t, sister), (g, prev, r), (g, later, r)):
        pl.semaphore_signal(barrier, inc=1, device_id=other, device_id_type=MESH)
    pl.semaphore_wait(barrier, 3)

    def remote(index, src, dst, device):
        return pltpu.make_async_remote_copy(
            src_ref=src,
            dst_ref=dst,
            send_sem=send_sem.at[index],
            recv_sem=recv_sem.at[index],
            device_id=device,
            device_id_type=MESH,
        )

    rim_start = pl.multiple_of((rows - REACH) * cols * (1 - r), 16)
    rest_start = pl.multiple_of(rim * r, 16)
    halo_there = pl.multiple_of((REACH + rows) * cols * r, 16)
    halo_zero = pl.multiple_of((REACH + rows) * cols * r, 16)
    rim_mine = pl.multiple_of(first + rim_start, 16)
    rest_mine = pl.multiple_of(first + rest_start, 16)

    own_halo = remote(
        0, x_ref.at[pl.ds(rim_start, rim)], own.at[pl.ds(halo_there, rim)], (g, t, sister)
    )
    next_rim = remote(
        1, x_ref.at[pl.ds(rim_start, rim)], nxt.at[pl.ds(rim_mine, rim)], (g, prev, r)
    )
    next_rest = remote(
        2, x_ref.at[pl.ds(rest_start, rest)], nxt.at[pl.ds(rest_mine, rest)], (g, prev, r)
    )
    next_halo = remote(
        3, nxt.at[pl.ds(rim_mine, rim)], nxt.at[pl.ds(halo_there, rim)], (g, t, sister)
    )
    own_halo.start()
    next_rim.start()
    next_rest.start()

    own[pl.ds(halo_zero, rim), :] = jnp.zeros((rim, channels), own.dtype)
    nxt[pl.ds(halo_zero, rim), :] = jnp.zeros((rim, channels), nxt.dtype)
    edge = HEAD_REACH * cols
    edge_zero = pl.multiple_of((HEAD_REACH + rows) * cols * r, 16)
    projected[pl.ds(edge_zero, edge), :] = jnp.zeros((edge, channels), projected.dtype)
    head_taps, head_width = head_hbm.shape[0], head_hbm.shape[1]
    head_w[:, pl.ds(head_width, LANES - head_width), :] = jnp.zeros(
        (head_taps, LANES - head_width, channels), head_w.dtype
    )

    label = label_ref[...]
    ids = lax.broadcasted_iota(jnp.int32, (LANES, cells), 0)
    onehot = jnp.where((ids == label) & (label > 0), 1.0, 0.0).astype(jnp.bfloat16)
    band_top = (r * rows).astype(jnp.float32)
    kind = lax.broadcasted_iota(jnp.int32, (8, cells), 0)
    place = place_ref[...] + jnp.where(kind == 1, band_top, 0.0)
    stats = dot_nt(place.astype(jnp.bfloat16), onehot)
    copies[0].wait()
    ones = jnp.ones((8, cells), jnp.bfloat16)
    channel_sums = dot_nn(ones, own[pl.ds(first, cells), :])
    small[:, :LANES] = stats
    small[:, LANES:] = channel_sums
    swap = remote(4, small, small_in, (g, t, sister))
    swap.start()
    swap.wait()
    total[...] = small[:, LANES:] + small_in[:, LANES:]
    frame_total = remote(5, total, total_in, (g, prev, r))
    frame_total.start()
    full_stats = small[:, :LANES] + small_in[:, :LANES]
    means = full_stats / jnp.maximum(full_stats[0:1], 1.0)
    high = means.astype(jnp.bfloat16)
    left = means - high.astype(jnp.float32)
    middle = left.astype(jnp.bfloat16)
    low = (left - middle.astype(jnp.float32)).astype(jnp.bfloat16)
    centre = dot_nn(high, onehot) + (dot_nn(middle, onehot) + dot_nn(low, onehot))
    aim = centre - place
    square = aim * aim
    counted = label > 0
    heat = jnp.where(
        counted,
        jnp.exp(-(square[1:2] + square[2:3]) / (2.0 * center_sigma * center_sigma)),
        0.0,
    )
    aux[...] = jnp.where(kind == 0, heat, aim)

    for copy in copies[1:]:
        copy.wait()

    col = lax.broadcasted_iota(jnp.int32, (tile_rows, cols, LANES), 1).reshape(tile, LANES)

    def widened(mask, width):
        return jnp.concatenate([mask] * (width // LANES), axis=1)

    def moved(value, step):
        width = value.shape[1]
        turned = pltpu.roll(value, (-step) % tile, 0)
        if step > 0:
            keep = col < cols - step
        else:
            keep = col >= -step
        return jnp.where(widened(keep, width), turned, 0.0)

    def branch_sums(source, base, part):
        lanes = pl.ds(part * channels, channels)
        centre_rows = source[pl.ds(pl.multiple_of(base, 16), tile), :]
        results = [dot_nt(centre_rows, point_w[:, lanes])]
        for b, spread in enumerate(DILATIONS):
            window = jnp.concatenate(
                [
                    source[pl.ds(pl.multiple_of(base - spread * cols, 16), tile), :],
                    centre_rows,
                    source[pl.ds(pl.multiple_of(base + spread * cols, 16), tile), :],
                ],
                axis=1,
            )
            value = None
            for j in (0, -1, 1):
                taps = jnp.concatenate(
                    [dilated_w[9 * b + 3 * i + j + 1, :, lanes] for i in range(3)], axis=1
                )
                piece = dot_nt(window, taps)
                if j != 0:
                    piece = moved(piece, j * spread)
                value = piece if value is None else value + piece
            results.append(value)
        return results

    own_halo.wait()

    def own_tile(k, carry):
        base = first + k * tile
        for b, value in enumerate(branch_sums(own, base, 0)):
            acc[b, pl.ds(pl.multiple_of(k * tile, 16), tile), :] = value
        return carry

    lax.fori_loop(0, tiles, own_tile, 0)

    next_rim.wait_recv()
    next_halo.start()

    frame_total.wait()
    clip_end = flag_ref[0, 0] == 1
    later_total = jnp.where(clip_end, total[...], total_in[...])
    pooled = jnp.concatenate(
        [
            (total[...] / (2.0 * cells)).astype(jnp.bfloat16),
            (later_total / (2.0 * cells)).astype(jnp.bfloat16),
        ],
        axis=1,
    )
    feature = jnp.maximum(dot_nt(pooled, pool_w[...]), 0.0).astype(jnp.bfloat16)
    width = point_w.shape[0]
    bias = dot_nt(feature, proj_w[:, pl.ds(4 * width, width)])[0:1]

    next_rim.wait_send()
    next_rest.wait()
    next_halo.wait()

    @pl.loop(0, (rows + 2 * REACH) // 4)
    def _(k):
        spot = pl.ds(pl.multiple_of(k * 4 * cols, 16), 4 * cols)
        nxt[spot, :] = jnp.where(clip_end, own[spot, :], nxt[spot, :])

    edge_src = pl.multiple_of((HEAD_REACH + (rows - HEAD_REACH) * (1 - r)) * cols, 16)
    edge_dst = pl.multiple_of((HEAD_REACH + rows) * cols * r, 16)
    edge_copy = remote(
        6,
        projected.at[pl.ds(edge_src, edge)],
        projected.at[pl.ds(edge_dst, edge)],
        (g, t, sister),
    )

    def next_tile(s, carry):
        k = r * s + (1 - r) * (tiles - 1 - s)
        base = first + k * tile
        spot = pl.ds(pl.multiple_of(k * tile, 16), tile)
        mixed = bias
        for b, value in enumerate(branch_sums(nxt, base, 1)):
            branch = jnp.maximum(value + acc[b, spot, :], 0.0).astype(jnp.bfloat16)
            mixed = mixed + dot_nt(branch, proj_w[:, pl.ds(b * width, width)])
        projected[pl.ds(pl.multiple_of((HEAD_REACH * cols) + k * tile, 16), tile), :] = jnp.maximum(
            mixed, 0.0
        ).astype(jnp.bfloat16)

        @pl.when(s == 0)
        def _():
            edge_copy.start()

        return carry

    lax.fori_loop(0, tiles, next_tile, 0)
    edge_copy.wait()

    size = 2 * HEAD_REACH + 1

    def head_tile(k, carry):
        base = HEAD_REACH * cols + k * tile
        window = jnp.concatenate(
            [
                projected[pl.ds(pl.multiple_of(base + (i - HEAD_REACH) * cols, 16), tile), :]
                for i in range(size)
            ],
            axis=1,
        )
        value = None
        for j in range(size):
            taps = jnp.concatenate([head_w[size * i + j] for i in range(size)], axis=1)
            piece = dot_nt(window, taps)
            if j != HEAD_REACH:
                piece = moved(piece, j - HEAD_REACH)
            value = piece if value is None else value + piece
        head = jnp.maximum(value, 0.0).astype(jnp.bfloat16)
        pred_ref[:, pl.ds(pl.multiple_of(k * tile, LANES), tile)] = dot_nt(out_w_ref[...], head)
        return carry

    lax.fori_loop(0, tiles, head_tile, 0)

    gap = pred_ref[...] - aux[...]
    center_err = jnp.sum(jnp.where(kind == 0, gap * gap, 0.0))
    offset_err = jnp.sum(jnp.where(((kind == 1) | (kind == 2)) & counted, jnp.abs(gap), 0.0))
    number = jnp.sum(jnp.where(counted, 1.0, 0.0))
    lane = lax.broadcasted_iota(jnp.int32, (8, LANES), 1)
    sums_ref[...] = jnp.where(
        lane == 0,
        center_err,
        jnp.where(lane == 1, offset_err, jnp.where(lane == 2, number, 0.0)),
    )


def shards(
    frames,
    clip_start,
    semantic,
    instance,
    aspp_point,
    aspp_dilated,
    pool_weight,
    proj_weight,
    head_weight,
    out_weight,
):
    _, channels, rows, cols = frames.shape
    cells = rows * cols
    frame_count = clip_start.shape[0]
    height = rows * lax.axis_size("row")
    width = aspp_point.shape[0]
    tile_rows = 8
    x = frames[0].reshape(channels, cells).T
    ahead = (lax.axis_index("tm") + 1) % frame_count
    flag = lax.dynamic_slice_in_dim(clip_start, ahead, 1).reshape(1, 1)
    label = jnp.where(semantic[0] >= THING_FIRST, instance[0], 0).reshape(1, cells)
    place = np.zeros((8, cells), np.float32)
    place[0] = 1.0
    place[1] = np.arange(cells) // cols
    place[2] = np.arange(cells) % cols
    part = out_weight.shape[1]
    group = np.minimum((np.arange(8) + 1) // 2, 2)
    out_w = jnp.where(
        np.arange(LANES)[None] // part == group[:, None],
        jnp.tile(jnp.pad(out_weight, ((0, 4), (0, 0))), (1, LANES // part)),
        0,
    )
    vmem = pl.BlockSpec(memory_space=pltpu.VMEM)
    anywhere = pl.BlockSpec(memory_space=pl.ANY)
    taps = aspp_dilated.shape[0] * aspp_dilated.shape[1]
    head_taps = head_weight.shape[0]
    tall = cells + 2 * REACH * cols
    bf16, f32 = jnp.bfloat16, jnp.float32
    pred, sums = pl.pallas_call(
        functools.partial(kernel, frame_count, rows, cols, tile_rows),
        out_shape=(
            jax.ShapeDtypeStruct((8, cells), f32),
            jax.ShapeDtypeStruct((8, LANES), f32),
        ),
        in_specs=[
            anywhere,
            pl.BlockSpec(memory_space=pltpu.SMEM),
            vmem,
            vmem,
            anywhere,
            anywhere,
            anywhere,
            anywhere,
            anywhere,
            vmem,
        ],
        out_specs=(vmem, vmem),
        scratch_shapes=[
            pltpu.VMEM((tall, channels), bf16),
            pltpu.VMEM((tall, channels), bf16),
            pltpu.VMEM((4, cells, width), f32),
            pltpu.VMEM(aspp_point.shape, bf16),
            pltpu.VMEM((taps,) + aspp_dilated.shape[2:], bf16),
            pltpu.VMEM(pool_weight.shape, bf16),
            pltpu.VMEM(proj_weight.shape, bf16),
            pltpu.VMEM((head_taps, LANES, width), bf16),
            pltpu.VMEM((cells + 2 * HEAD_REACH * cols, width), bf16),
            pltpu.VMEM((8, cells), f32),
            pltpu.VMEM((8, LANES + channels), f32),
            pltpu.VMEM((8, LANES + channels), f32),
            pltpu.VMEM((8, channels), f32),
            pltpu.VMEM((8, channels), f32),
            pltpu.SemaphoreType.DMA((6,)),
            pltpu.SemaphoreType.DMA((7,)),
            pltpu.SemaphoreType.DMA((7,)),
        ],
        compiler_params=pltpu.CompilerParams(
            collective_id=0, has_side_effects=True, vmem_limit_bytes=56 * 1024 * 1024
        ),
    )(
        x,
        flag,
        label,
        jnp.asarray(place),
        aspp_point,
        aspp_dilated.reshape((taps,) + aspp_dilated.shape[2:]),
        pool_weight,
        proj_weight,
        head_weight,
        out_w,
    )
    predictions = pred[:4].reshape(1, 4, rows, cols)
    totals = lax.psum(sums[0, :3], ("tm", "row"))
    losses = jnp.stack(
        [
            totals[0] / (frame_count * height * cols),
            offset_weight * totals[1] / jnp.maximum(totals[2], 1.0),
        ]
    )
    return (predictions, losses)


def solution(mesh):
    placed = (
        P(("grp", "tm"), None, "row", None),
        P("grp"),
        P(("grp", "tm"), "row", None),
        P(("grp", "tm"), "row", None),
        P(),
        P(),
        P(),
        P(),
        P(),
        P(),
    )
    return jax.shard_map(
        shards,
        mesh=mesh,
        in_specs=placed,
        out_specs=(P(("grp", "tm"), None, "row", None), P("grp")),
        check_vma=False,
    )
```

```python
import functools

import jax
import jax.numpy as jnp
from jax import lax
from jax.experimental import pallas as pl
from jax.experimental.pallas import tpu as pltpu
from jax.sharding import PartitionSpec as P

THING_FIRST = 11
DILATIONS = (6, 12, 18)
REACH = 18
HEAD_REACH = 2
LANES = 128
center_sigma = 8.0
offset_weight = 0.01
MESH = pl.DeviceIdType.MESH


def dot_nt(a, b):
    return lax.dot_general(a, b, (((1,), (1,)), ((), ())), preferred_element_type=jnp.float32)


def dot_nn(a, b):
    return lax.dot_general(a, b, (((1,), (0,)), ((), ())), preferred_element_type=jnp.float32)


def kernel(
    frame_count,
    rows,
    cols,
    tile_rows,
    x_ref,
    clip_ref,
    semantic_ref,
    instance_ref,
    point_hbm,
    dilated_hbm,
    pool_hbm,
    proj_hbm,
    head_hbm,
    out_w_ref,
    pred_ref,
    losses_ref,
    own,
    nxt,
    acc,
    point_w,
    dilated_w,
    pool_w,
    proj_w,
    head_w,
    projected,
    heat_map,
    aim_map,
    out_full,
    small,
    small_in,
    total,
    total_in,
    err,
    err_in,
    err_pair,
    err_all,
    local_sem,
    send_sem,
    recv_sem,
    all_send_sem,
    all_recv_sem,
):
    g = lax.axis_index("grp")
    t = lax.axis_index("tm")
    r = lax.axis_index("row")
    prev = lax.rem(t + frame_count - 1, frame_count)
    later = lax.rem(t + 1, frame_count)
    sister = 1 - r
    cells = rows * cols
    tile = tile_rows * cols
    tiles = rows // tile_rows
    first = REACH * cols
    channels = x_ref.shape[1]
    rim = REACH * cols
    rest = cells - rim

    def local(index, src, dst):
        return pltpu.make_async_copy(src, dst, local_sem.at[index])

    copies = [
        local(0, x_ref, own.at[pl.ds(first, cells)]),
        local(1, dilated_hbm, dilated_w),
        local(2, point_hbm, point_w),
        local(3, pool_hbm, pool_w),
        local(4, proj_hbm, proj_w),
        local(5, head_hbm, head_w.at[:, pl.ds(0, head_hbm.shape[1])]),
    ]
    for copy in copies:
        copy.start()

    barrier = pltpu.get_barrier_semaphore()
    others = [lax.rem(t + step, frame_count) for step in range(1, frame_count)]
    for other in [(g, t, sister)] + [(g, frame, r) for frame in others]:
        pl.semaphore_signal(barrier, inc=1, device_id=other, device_id_type=MESH)
    pl.semaphore_wait(barrier, frame_count)

    def remote(index, src, dst, device):
        return pltpu.make_async_remote_copy(
            src_ref=src,
            dst_ref=dst,
            send_sem=send_sem.at[index],
            recv_sem=recv_sem.at[index],
            device_id=device,
            device_id_type=MESH,
        )

    rim_start = pl.multiple_of((rows - REACH) * cols * (1 - r), 16)
    rest_start = pl.multiple_of(rim * r, 16)
    halo_there = pl.multiple_of((REACH + rows) * cols * r, 16)
    halo_zero = pl.multiple_of((REACH + rows) * cols * r, 16)
    rim_mine = pl.multiple_of(first + rim_start, 16)
    rest_mine = pl.multiple_of(first + rest_start, 16)

    own_halo = remote(
        0, x_ref.at[pl.ds(rim_start, rim)], own.at[pl.ds(halo_there, rim)], (g, t, sister)
    )
    next_rim = remote(
        1, x_ref.at[pl.ds(rim_start, rim)], nxt.at[pl.ds(rim_mine, rim)], (g, prev, r)
    )
    next_rest = remote(
        2, x_ref.at[pl.ds(rest_start, rest)], nxt.at[pl.ds(rest_mine, rest)], (g, prev, r)
    )
    next_halo = remote(
        3, nxt.at[pl.ds(rim_mine, rim)], nxt.at[pl.ds(halo_there, rim)], (g, t, sister)
    )
    own_halo.start()
    next_rim.start()
    next_rest.start()

    own[pl.ds(halo_zero, rim), :] = jnp.zeros((rim, channels), own.dtype)
    nxt[pl.ds(halo_zero, rim), :] = jnp.zeros((rim, channels), nxt.dtype)
    edge = HEAD_REACH * cols
    edge_zero = pl.multiple_of((HEAD_REACH + rows) * cols * r, 16)
    projected[pl.ds(edge_zero, edge), :] = jnp.zeros((edge, channels), projected.dtype)
    head_taps, head_width = head_hbm.shape[0], head_hbm.shape[1]
    head_w[:, pl.ds(head_width, LANES - head_width), :] = jnp.zeros(
        (head_taps, LANES - head_width, channels), head_w.dtype
    )

    shape = (8, cols)
    ids = lax.broadcasted_iota(jnp.int32, (LANES, cols), 0)
    kind = lax.broadcasted_iota(jnp.int32, shape, 0)
    across = lax.broadcasted_iota(jnp.int32, shape, 1).astype(jnp.float32)
    band_top = r * rows
    label = jnp.where(semantic_ref[0] >= THING_FIRST, instance_ref[0], 0)

    def onehot_row(y):
        row = label[y : y + 1]
        return jnp.where((ids == row) & (row > 0), 1.0, 0.0).astype(jnp.bfloat16)

    def place_row(y):
        down = (band_top + y).astype(jnp.float32)
        return jnp.where(kind == 0, 1.0, jnp.where(kind == 1, down, across))

    stats = jnp.zeros((8, LANES), jnp.float32)
    for y in range(rows):
        stats = stats + dot_nt(place_row(y).astype(jnp.bfloat16), onehot_row(y))
    copies[0].wait()
    ones = jnp.ones((8, cells), jnp.bfloat16)
    channel_sums = dot_nn(ones, own[pl.ds(first, cells), :])
    small[:, :LANES] = stats
    small[:, LANES:] = channel_sums
    swap = remote(4, small, small_in, (g, t, sister))
    swap.start()
    swap.wait()
    total[...] = small[:, LANES:] + small_in[:, LANES:]
    frame_total = remote(5, total, total_in, (g, prev, r))
    frame_total.start()
    full_stats = small[:, :LANES] + small_in[:, :LANES]
    means = full_stats / jnp.maximum(full_stats[0:1], 1.0)
    high = means.astype(jnp.bfloat16)
    left = means - high.astype(jnp.float32)
    middle = left.astype(jnp.bfloat16)
    low = (left - middle.astype(jnp.float32)).astype(jnp.bfloat16)
    parts = jnp.concatenate([high, middle, low], axis=0)
    for top in range(0, rows, 8):
        aims = []
        for y in range(top, top + 8):
            centre = dot_nn(parts, onehot_row(y))
            aims.append(centre[0:8] + (centre[8:16] + centre[16:24]) - place_row(y))
        for axis in range(2):
            aim_map[axis, pl.ds(top, 8), :] = jnp.concatenate(
                [aim[axis + 1 : axis + 2] for aim in aims], axis=0
            )
    counted = label > 0
    square = aim_map[0] * aim_map[0] + aim_map[1] * aim_map[1]
    heat_map[...] = jnp.where(
        counted, jnp.exp(-square / (2.0 * center_sigma * center_sigma)), 0.0
    )

    part = out_w_ref.shape[1]
    out_full[...] = jnp.zeros(out_full.shape, jnp.float32)
    plain = out_w_ref[...].astype(jnp.float32)
    wide = jnp.concatenate([plain] * (LANES // part), axis=1)
    channel = lax.broadcasted_iota(jnp.int32, wide.shape, 0)
    group = lax.broadcasted_iota(jnp.int32, wide.shape, 1) // part
    out_full[pl.ds(0, 4), :] = jnp.where(group == (channel + 1) // 2, wide, 0.0)

    for copy in copies[1:]:
        copy.wait()

    col = lax.broadcasted_iota(jnp.int32, (tile_rows, cols, LANES), 1).reshape(tile, LANES)

    def widened(mask, width):
        return jnp.concatenate([mask] * (width // LANES), axis=1)

    def moved(value, step):
        width = value.shape[1]
        turned = pltpu.roll(value, (-step) % tile, 0)
        if step > 0:
            keep = col < cols - step
        else:
            keep = col >= -step
        return jnp.where(widened(keep, width), turned, 0.0)

    def branch_sums(source, base, part):
        lanes = pl.ds(part * channels, channels)
        centre_rows = source[pl.ds(pl.multiple_of(base, 16), tile), :]
        results = [dot_nt(centre_rows, point_w[:, lanes])]
        for b, spread in enumerate(DILATIONS):
            window = jnp.concatenate(
                [
                    source[pl.ds(pl.multiple_of(base - spread * cols, 16), tile), :],
                    centre_rows,
                    source[pl.ds(pl.multiple_of(base + spread * cols, 16), tile), :],
                ],
                axis=1,
            )
            value = None
            for j in (0, -1, 1):
                taps = jnp.concatenate(
                    [dilated_w[9 * b + 3 * i + j + 1, :, lanes] for i in range(3)], axis=1
                )
                piece = dot_nt(window, taps)
                if j != 0:
                    piece = moved(piece, j * spread)
                value = piece if value is None else value + piece
            results.append(value)
        return results

    own_halo.wait()

    def own_tile(k, carry):
        base = first + k * tile
        for b, value in enumerate(branch_sums(own, base, 0)):
            acc[b, pl.ds(pl.multiple_of(k * tile, 16), tile), :] = value
        return carry

    lax.fori_loop(0, tiles, own_tile, 0)

    next_rim.wait_recv()
    next_halo.start()

    frame_total.wait()
    clip_end = clip_ref[later] == 1
    later_total = jnp.where(clip_end, total[...], total_in[...])
    pooled = jnp.concatenate(
        [
            (total[...] / (2.0 * cells)).astype(jnp.bfloat16),
            (later_total / (2.0 * cells)).astype(jnp.bfloat16),
        ],
        axis=1,
    )
    feature = jnp.maximum(dot_nt(pooled, pool_w[...]), 0.0).astype(jnp.bfloat16)
    width = point_w.shape[0]
    bias = dot_nt(feature, proj_w[:, pl.ds(4 * width, width)])[0:1]

    next_rim.wait_send()
    next_rest.wait()
    next_halo.wait()

    @pl.loop(0, (rows + 2 * REACH) // 4)
    def _(k):
        spot = pl.ds(pl.multiple_of(k * 4 * cols, 16), 4 * cols)
        nxt[spot, :] = jnp.where(clip_end, own[spot, :], nxt[spot, :])

    edge_src = pl.multiple_of((HEAD_REACH + (rows - HEAD_REACH) * (1 - r)) * cols, 16)
    edge_dst = pl.multiple_of((HEAD_REACH + rows) * cols * r, 16)
    edge_copy = remote(
        6,
        projected.at[pl.ds(edge_src, edge)],
        projected.at[pl.ds(edge_dst, edge)],
        (g, t, sister),
    )

    def next_tile(s, carry):
        k = r * s + (1 - r) * (tiles - 1 - s)
        base = first + k * tile
        spot = pl.ds(pl.multiple_of(k * tile, 16), tile)
        mixed = bias
        for b, value in enumerate(branch_sums(nxt, base, 1)):
            branch = jnp.maximum(value + acc[b, spot, :], 0.0).astype(jnp.bfloat16)
            mixed = mixed + dot_nt(branch, proj_w[:, pl.ds(b * width, width)])
        projected[pl.ds(pl.multiple_of((HEAD_REACH * cols) + k * tile, 16), tile), :] = jnp.maximum(
            mixed, 0.0
        ).astype(jnp.bfloat16)

        @pl.when(s == 0)
        def _():
            edge_copy.start()

        return carry

    lax.fori_loop(0, tiles, next_tile, 0)
    edge_copy.wait()

    size = 2 * HEAD_REACH + 1

    def head_tile(k, carry):
        base = HEAD_REACH * cols + k * tile
        window = jnp.concatenate(
            [
                projected[pl.ds(pl.multiple_of(base + (i - HEAD_REACH) * cols, 16), tile), :]
                for i in range(size)
            ],
            axis=1,
        )
        value = None
        for j in range(size):
            taps = jnp.concatenate([head_w[size * i + j] for i in range(size)], axis=1)
            piece = dot_nt(window, taps)
            if j != HEAD_REACH:
                piece = moved(piece, j - HEAD_REACH)
            value = piece if value is None else value + piece
        head = jnp.maximum(value, 0.0).astype(jnp.bfloat16)
        weights = out_full[...].astype(jnp.bfloat16)
        maps = [
            dot_nt(weights, head[y * cols : (y + 1) * cols]) for y in range(tile_rows)
        ]
        for c in range(4):
            pred_ref[0, c, pl.ds(pl.multiple_of(k * tile_rows, 8), tile_rows), :] = (
                jnp.concatenate([value[c : c + 1] for value in maps], axis=0)
            )
        return carry

    lax.fori_loop(0, tiles, head_tile, 0)

    gap = pred_ref[0, 0] - heat_map[...]
    offset_gap = jnp.abs(pred_ref[0, 1] - aim_map[0]) + jnp.abs(pred_ref[0, 2] - aim_map[1])
    err[...] = jnp.zeros(err.shape, jnp.float32)
    err[0:1, pl.ds(0, cols)] = jnp.sum(gap * gap, axis=0, keepdims=True)
    err[1:2, pl.ds(0, cols)] = jnp.sum(
        jnp.where(counted, offset_gap, 0.0), axis=0, keepdims=True
    )
    err[2:3, pl.ds(0, cols)] = jnp.sum(jnp.where(counted, 1.0, 0.0), axis=0, keepdims=True)
    pair = remote(7, err, err_in, (g, t, sister))
    pair.start()
    pair.wait()
    err_pair[...] = err[...] + err_in[...]
    err_all[t] = err_pair[...]

    def spread_copy(step, slot):
        return pltpu.make_async_remote_copy(
            src_ref=err_pair,
            dst_ref=err_all.at[slot],
            send_sem=all_send_sem.at[step],
            recv_sem=all_recv_sem.at[slot],
            device_id=(g, others[step], r),
            device_id_type=MESH,
        )

    for step in range(frame_count - 1):
        spread_copy(step, t).start()
    for step in range(frame_count - 1):
        spread_copy(step, t).wait_send()
        spread_copy(step, others[step]).wait_recv()
    summed = err_all[0]
    for frame in range(1, frame_count):
        summed = summed + err_all[frame]
    sums = jnp.sum(summed, axis=1, keepdims=True)
    center_loss = sums[0:1] / (frame_count * 2 * cells)
    offset_loss = offset_weight * sums[1:2] / jnp.maximum(sums[2:3], 1.0)
    losses_ref[0] = center_loss[0, 0]
    losses_ref[1] = offset_loss[0, 0]


def shards(
    frames,
    clip_start,
    semantic,
    instance,
    aspp_point,
    aspp_dilated,
    pool_weight,
    proj_weight,
    head_weight,
    out_weight,
):
    _, channels, rows, cols = frames.shape
    cells = rows * cols
    frame_count = clip_start.shape[0]
    width = aspp_point.shape[0]
    tile_rows = 8
    x = frames[0].reshape(channels, cells).T
    vmem = pl.BlockSpec(memory_space=pltpu.VMEM)
    anywhere = pl.BlockSpec(memory_space=pl.ANY)
    taps = aspp_dilated.shape[0] * aspp_dilated.shape[1]
    head_taps = head_weight.shape[0]
    tall = cells + 2 * REACH * cols
    bf16, f32 = jnp.bfloat16, jnp.float32
    return pl.pallas_call(
        functools.partial(kernel, frame_count, rows, cols, tile_rows),
        out_shape=(
            jax.ShapeDtypeStruct((1, 4, rows, cols), f32),
            jax.ShapeDtypeStruct((2,), f32),
        ),
        in_specs=[
            anywhere,
            pl.BlockSpec(memory_space=pltpu.SMEM),
            vmem,
            vmem,
            anywhere,
            anywhere,
            anywhere,
            anywhere,
            anywhere,
            vmem,
        ],
        out_specs=(vmem, pl.BlockSpec(memory_space=pltpu.SMEM)),
        scratch_shapes=[
            pltpu.VMEM((tall, channels), bf16),
            pltpu.VMEM((tall, channels), bf16),
            pltpu.VMEM((4, cells, width), f32),
            pltpu.VMEM(aspp_point.shape, bf16),
            pltpu.VMEM((taps,) + aspp_dilated.shape[2:], bf16),
            pltpu.VMEM(pool_weight.shape, bf16),
            pltpu.VMEM(proj_weight.shape, bf16),
            pltpu.VMEM((head_taps, LANES, width), bf16),
            pltpu.VMEM((cells + 2 * HEAD_REACH * cols, width), bf16),
            pltpu.VMEM((rows, cols), f32),
            pltpu.VMEM((2, rows, cols), f32),
            pltpu.VMEM((8, LANES), f32),
            pltpu.VMEM((8, LANES + channels), f32),
            pltpu.VMEM((8, LANES + channels), f32),
            pltpu.VMEM((8, channels), f32),
            pltpu.VMEM((8, channels), f32),
            pltpu.VMEM((8, LANES), f32),
            pltpu.VMEM((8, LANES), f32),
            pltpu.VMEM((8, LANES), f32),
            pltpu.VMEM((frame_count, 8, LANES), f32),
            pltpu.SemaphoreType.DMA((6,)),
            pltpu.SemaphoreType.DMA((8,)),
            pltpu.SemaphoreType.DMA((8,)),
            pltpu.SemaphoreType.DMA((frame_count - 1,)),
            pltpu.SemaphoreType.DMA((frame_count,)),
        ],
        compiler_params=pltpu.CompilerParams(
            collective_id=0, has_side_effects=True, vmem_limit_bytes=56 * 1024 * 1024
        ),
    )(
        x,
        clip_start,
        semantic,
        instance,
        aspp_point,
        aspp_dilated.reshape((taps,) + aspp_dilated.shape[2:]),
        pool_weight,
        proj_weight,
        head_weight,
        out_weight,
    )


def solution(mesh):
    placed = (
        P(("grp", "tm"), None, "row", None),
        P("grp"),
        P(("grp", "tm"), "row", None),
        P(("grp", "tm"), "row", None),
        P(),
        P(),
        P(),
        P(),
        P(),
        P(),
    )
    return jax.shard_map(
        shards,
        mesh=mesh,
        in_specs=placed,
        out_specs=(P(("grp", "tm"), None, "row", None), P("grp")),
        check_vma=False,
    )
```

```python
import functools

import jax
import jax.numpy as jnp
import numpy as np
from jax import lax
from jax.experimental import pallas as pl
from jax.experimental.pallas import tpu as pltpu
from jax.sharding import PartitionSpec as P

THING_FIRST = 11
DILATIONS = (6, 12, 18)
REACH = 18
HEAD_REACH = 2
LANES = 128
center_sigma = 8.0
offset_weight = 0.01
MESH = pl.DeviceIdType.MESH


def dot_nt(a, b):
    return lax.dot_general(a, b, (((1,), (1,)), ((), ())), preferred_element_type=jnp.float32)


def dot_nn(a, b):
    return lax.dot_general(a, b, (((1,), (0,)), ((), ())), preferred_element_type=jnp.float32)


def kernel(
    frame_count,
    rows,
    cols,
    tile_rows,
    x_ref,
    clip_ref,
    semantic_ref,
    instance_ref,
    place_ref,
    point_hbm,
    dilated_hbm,
    pool_hbm,
    proj_hbm,
    head_hbm,
    out_w_ref,
    pred_ref,
    losses_ref,
    own,
    nxt,
    acc,
    point_w,
    dilated_w,
    pool_w,
    proj_w,
    head_w,
    projected,
    heat_map,
    aim_map,
    out_full,
    small,
    small_in,
    total,
    total_in,
    err,
    err_in,
    err_pair,
    err_all,
    local_sem,
    send_sem,
    recv_sem,
    all_send_sem,
    all_recv_sem,
):
    g = lax.axis_index("grp")
    t = lax.axis_index("tm")
    r = lax.axis_index("row")
    prev = lax.rem(t + frame_count - 1, frame_count)
    later = lax.rem(t + 1, frame_count)
    sister = 1 - r
    cells = rows * cols
    tile = tile_rows * cols
    tiles = rows // tile_rows
    first = REACH * cols
    channels = x_ref.shape[1]
    rim = REACH * cols
    rest = cells - rim

    def local(index, src, dst):
        return pltpu.make_async_copy(src, dst, local_sem.at[index])

    copies = [
        local(0, x_ref, own.at[pl.ds(first, cells)]),
        local(1, dilated_hbm, dilated_w),
        local(2, point_hbm, point_w),
        local(3, pool_hbm, pool_w),
        local(4, proj_hbm, proj_w),
        local(5, head_hbm, head_w.at[:, pl.ds(0, head_hbm.shape[1])]),
    ]
    for copy in copies:
        copy.start()

    barrier = pltpu.get_barrier_semaphore()
    others = [lax.rem(t + step, frame_count) for step in range(1, frame_count)]
    for other in [(g, t, sister)] + [(g, frame, r) for frame in others]:
        pl.semaphore_signal(barrier, inc=1, device_id=other, device_id_type=MESH)
    pl.semaphore_wait(barrier, frame_count)

    def remote(index, src, dst, device):
        return pltpu.make_async_remote_copy(
            src_ref=src,
            dst_ref=dst,
            send_sem=send_sem.at[index],
            recv_sem=recv_sem.at[index],
            device_id=device,
            device_id_type=MESH,
        )

    rim_start = pl.multiple_of((rows - REACH) * cols * (1 - r), 16)
    rest_start = pl.multiple_of(rim * r, 16)
    halo_there = pl.multiple_of((REACH + rows) * cols * r, 16)
    halo_zero = pl.multiple_of((REACH + rows) * cols * r, 16)
    rim_mine = pl.multiple_of(first + rim_start, 16)
    rest_mine = pl.multiple_of(first + rest_start, 16)

    own_halo = remote(
        0, x_ref.at[pl.ds(rim_start, rim)], own.at[pl.ds(halo_there, rim)], (g, t, sister)
    )
    next_rim = remote(
        1, x_ref.at[pl.ds(rim_start, rim)], nxt.at[pl.ds(rim_mine, rim)], (g, prev, r)
    )
    next_rest = remote(
        2, x_ref.at[pl.ds(rest_start, rest)], nxt.at[pl.ds(rest_mine, rest)], (g, prev, r)
    )
    next_halo = remote(
        3, nxt.at[pl.ds(rim_mine, rim)], nxt.at[pl.ds(halo_there, rim)], (g, t, sister)
    )
    own_halo.start()
    next_rim.start()
    next_rest.start()

    own[pl.ds(halo_zero, rim), :] = jnp.zeros((rim, channels), own.dtype)
    nxt[pl.ds(halo_zero, rim), :] = jnp.zeros((rim, channels), nxt.dtype)
    edge = HEAD_REACH * cols
    edge_zero = pl.multiple_of((HEAD_REACH + rows) * cols * r, 16)
    projected[pl.ds(edge_zero, edge), :] = jnp.zeros((edge, channels), projected.dtype)
    head_taps, head_width = head_hbm.shape[0], head_hbm.shape[1]
    head_w[:, pl.ds(head_width, LANES - head_width), :] = jnp.zeros(
        (head_taps, LANES - head_width, channels), head_w.dtype
    )

    label = jnp.where(semantic_ref[0] >= THING_FIRST, instance_ref[0], 0)
    flat = jnp.concatenate([label[y : y + 1] for y in range(rows)], axis=1)
    ids = lax.broadcasted_iota(jnp.int32, (LANES, cells), 0)
    onehot = jnp.where((ids == flat) & (flat > 0), 1.0, 0.0).astype(jnp.bfloat16)
    band_top = (r * rows).astype(jnp.float32)
    kind = lax.broadcasted_iota(jnp.int32, (8, cells), 0)
    place = place_ref[...] + jnp.where(kind == 1, band_top, 0.0)
    stats = dot_nt(place.astype(jnp.bfloat16), onehot)
    copies[0].wait()
    ones = jnp.ones((8, cells), jnp.bfloat16)
    channel_sums = dot_nn(ones, own[pl.ds(first, cells), :])
    small[:, :LANES] = stats
    small[:, LANES:] = channel_sums
    swap = remote(4, small, small_in, (g, t, sister))
    swap.start()
    swap.wait()
    total[...] = small[:, LANES:] + small_in[:, LANES:]
    frame_total = remote(5, total, total_in, (g, prev, r))
    frame_total.start()
    full_stats = small[:, :LANES] + small_in[:, :LANES]
    means = full_stats / jnp.maximum(full_stats[0:1], 1.0)
    high = means.astype(jnp.bfloat16)
    left = means - high.astype(jnp.float32)
    middle = left.astype(jnp.bfloat16)
    low = (left - middle.astype(jnp.float32)).astype(jnp.bfloat16)
    parts = jnp.concatenate([high, middle, low], axis=0)
    centre = dot_nn(parts, onehot)
    aim = centre[0:8] + (centre[8:16] + centre[16:24]) - place
    for axis in range(2):
        aim_map[axis] = jnp.concatenate(
            [aim[axis + 1 : axis + 2, y * cols : (y + 1) * cols] for y in range(rows)], axis=0
        )
    counted = label > 0
    square = aim_map[0] * aim_map[0] + aim_map[1] * aim_map[1]
    heat_map[...] = jnp.where(
        counted, jnp.exp(-square / (2.0 * center_sigma * center_sigma)), 0.0
    )

    part = out_w_ref.shape[1]
    out_full[...] = jnp.zeros(out_full.shape, jnp.float32)
    plain = out_w_ref[...].astype(jnp.float32)
    wide = jnp.concatenate([plain] * (LANES // part), axis=1)
    channel = lax.broadcasted_iota(jnp.int32, wide.shape, 0)
    group = lax.broadcasted_iota(jnp.int32, wide.shape, 1) // part
    out_full[pl.ds(0, 4), :] = jnp.where(group == (channel + 1) // 2, wide, 0.0)

    for copy in copies[1:]:
        copy.wait()

    col = lax.broadcasted_iota(jnp.int32, (tile_rows, cols, LANES), 1).reshape(tile, LANES)

    def widened(mask, width):
        return jnp.concatenate([mask] * (width // LANES), axis=1)

    def moved(value, step):
        width = value.shape[1]
        turned = pltpu.roll(value, (-step) % tile, 0)
        if step > 0:
            keep = col < cols - step
        else:
            keep = col >= -step
        return jnp.where(widened(keep, width), turned, 0.0)

    def branch_sums(source, base, part):
        lanes = pl.ds(part * channels, channels)
        centre_rows = source[pl.ds(pl.multiple_of(base, 16), tile), :]
        results = [dot_nt(centre_rows, point_w[:, lanes])]
        for b, spread in enumerate(DILATIONS):
            window = jnp.concatenate(
                [
                    source[pl.ds(pl.multiple_of(base - spread * cols, 16), tile), :],
                    centre_rows,
                    source[pl.ds(pl.multiple_of(base + spread * cols, 16), tile), :],
                ],
                axis=1,
            )
            value = None
            for j in (0, -1, 1):
                taps = jnp.concatenate(
                    [dilated_w[9 * b + 3 * i + j + 1, :, lanes] for i in range(3)], axis=1
                )
                piece = dot_nt(window, taps)
                if j != 0:
                    piece = moved(piece, j * spread)
                value = piece if value is None else value + piece
            results.append(value)
        return results

    own_halo.wait()

    def own_tile(k, carry):
        base = first + k * tile
        for b, value in enumerate(branch_sums(own, base, 0)):
            acc[b, pl.ds(pl.multiple_of(k * tile, 16), tile), :] = value
        return carry

    lax.fori_loop(0, tiles, own_tile, 0)

    next_rim.wait_recv()
    next_halo.start()

    frame_total.wait()
    clip_end = clip_ref[later] == 1
    later_total = jnp.where(clip_end, total[...], total_in[...])
    pooled = jnp.concatenate(
        [
            (total[...] / (2.0 * cells)).astype(jnp.bfloat16),
            (later_total / (2.0 * cells)).astype(jnp.bfloat16),
        ],
        axis=1,
    )
    feature = jnp.maximum(dot_nt(pooled, pool_w[...]), 0.0).astype(jnp.bfloat16)
    width = point_w.shape[0]
    bias = dot_nt(feature, proj_w[:, pl.ds(4 * width, width)])[0:1]

    next_rim.wait_send()
    next_rest.wait()
    next_halo.wait()

    @pl.loop(0, (rows + 2 * REACH) // 4)
    def _(k):
        spot = pl.ds(pl.multiple_of(k * 4 * cols, 16), 4 * cols)
        nxt[spot, :] = jnp.where(clip_end, own[spot, :], nxt[spot, :])

    edge_src = pl.multiple_of((HEAD_REACH + (rows - HEAD_REACH) * (1 - r)) * cols, 16)
    edge_dst = pl.multiple_of((HEAD_REACH + rows) * cols * r, 16)
    edge_copy = remote(
        6,
        projected.at[pl.ds(edge_src, edge)],
        projected.at[pl.ds(edge_dst, edge)],
        (g, t, sister),
    )

    def next_tile(s, carry):
        k = r * s + (1 - r) * (tiles - 1 - s)
        base = first + k * tile
        spot = pl.ds(pl.multiple_of(k * tile, 16), tile)
        mixed = bias
        for b, value in enumerate(branch_sums(nxt, base, 1)):
            branch = jnp.maximum(value + acc[b, spot, :], 0.0).astype(jnp.bfloat16)
            mixed = mixed + dot_nt(branch, proj_w[:, pl.ds(b * width, width)])
        projected[pl.ds(pl.multiple_of((HEAD_REACH * cols) + k * tile, 16), tile), :] = jnp.maximum(
            mixed, 0.0
        ).astype(jnp.bfloat16)

        @pl.when(s == 0)
        def _():
            edge_copy.start()

        return carry

    lax.fori_loop(0, tiles, next_tile, 0)
    edge_copy.wait()

    size = 2 * HEAD_REACH + 1

    def head_tile(k, carry):
        base = HEAD_REACH * cols + k * tile
        window = jnp.concatenate(
            [
                projected[pl.ds(pl.multiple_of(base + (i - HEAD_REACH) * cols, 16), tile), :]
                for i in range(size)
            ],
            axis=1,
        )
        value = None
        for j in range(size):
            taps = jnp.concatenate([head_w[size * i + j] for i in range(size)], axis=1)
            piece = dot_nt(window, taps)
            if j != HEAD_REACH:
                piece = moved(piece, j - HEAD_REACH)
            value = piece if value is None else value + piece
        head = jnp.maximum(value, 0.0).astype(jnp.bfloat16)
        weights = out_full[...].astype(jnp.bfloat16)
        maps = [
            dot_nt(weights, head[y * cols : (y + 1) * cols]) for y in range(tile_rows)
        ]
        for c in range(4):
            pred_ref[0, c, pl.ds(pl.multiple_of(k * tile_rows, 8), tile_rows), :] = (
                jnp.concatenate([value[c : c + 1] for value in maps], axis=0)
            )
        return carry

    lax.fori_loop(0, tiles, head_tile, 0)

    gap = pred_ref[0, 0] - heat_map[...]
    offset_gap = jnp.abs(pred_ref[0, 1] - aim_map[0]) + jnp.abs(pred_ref[0, 2] - aim_map[1])
    err[...] = jnp.zeros(err.shape, jnp.float32)
    err[0:1, pl.ds(0, cols)] = jnp.sum(gap * gap, axis=0, keepdims=True)
    err[1:2, pl.ds(0, cols)] = jnp.sum(
        jnp.where(counted, offset_gap, 0.0), axis=0, keepdims=True
    )
    err[2:3, pl.ds(0, cols)] = jnp.sum(jnp.where(counted, 1.0, 0.0), axis=0, keepdims=True)
    pair = remote(7, err, err_in, (g, t, sister))
    pair.start()
    pair.wait()
    err_pair[...] = err[...] + err_in[...]
    err_all[t] = err_pair[...]

    def spread_copy(step, slot):
        return pltpu.make_async_remote_copy(
            src_ref=err_pair,
            dst_ref=err_all.at[slot],
            send_sem=all_send_sem.at[step],
            recv_sem=all_recv_sem.at[slot],
            device_id=(g, others[step], r),
            device_id_type=MESH,
        )

    for step in range(frame_count - 1):
        spread_copy(step, t).start()
    for step in range(frame_count - 1):
        spread_copy(step, t).wait_send()
        spread_copy(step, others[step]).wait_recv()
    summed = err_all[0]
    for frame in range(1, frame_count):
        summed = summed + err_all[frame]
    sums = jnp.sum(summed, axis=1, keepdims=True)
    center_loss = sums[0:1] / (frame_count * 2 * cells)
    offset_loss = offset_weight * sums[1:2] / jnp.maximum(sums[2:3], 1.0)
    losses_ref[0] = center_loss[0, 0]
    losses_ref[1] = offset_loss[0, 0]


def shards(
    frames,
    clip_start,
    semantic,
    instance,
    aspp_point,
    aspp_dilated,
    pool_weight,
    proj_weight,
    head_weight,
    out_weight,
):
    _, channels, rows, cols = frames.shape
    cells = rows * cols
    frame_count = clip_start.shape[0]
    width = aspp_point.shape[0]
    tile_rows = 16
    place = np.zeros((8, cells), np.float32)
    place[0] = 1.0
    place[1] = np.arange(cells) // cols
    place[2] = np.arange(cells) % cols
    x = frames[0].reshape(channels, cells).T
    vmem = pl.BlockSpec(memory_space=pltpu.VMEM)
    anywhere = pl.BlockSpec(memory_space=pl.ANY)
    taps = aspp_dilated.shape[0] * aspp_dilated.shape[1]
    head_taps = head_weight.shape[0]
    tall = cells + 2 * REACH * cols
    bf16, f32 = jnp.bfloat16, jnp.float32
    return pl.pallas_call(
        functools.partial(kernel, frame_count, rows, cols, tile_rows),
        out_shape=(
            jax.ShapeDtypeStruct((1, 4, rows, cols), f32),
            jax.ShapeDtypeStruct((2,), f32),
        ),
        in_specs=[
            anywhere,
            pl.BlockSpec(memory_space=pltpu.SMEM),
            vmem,
            vmem,
            vmem,
            anywhere,
            anywhere,
            anywhere,
            anywhere,
            anywhere,
            vmem,
        ],
        out_specs=(vmem, pl.BlockSpec(memory_space=pltpu.SMEM)),
        scratch_shapes=[
            pltpu.VMEM((tall, channels), bf16),
            pltpu.VMEM((tall, channels), bf16),
            pltpu.VMEM((4, cells, width), f32),
            pltpu.VMEM(aspp_point.shape, bf16),
            pltpu.VMEM((taps,) + aspp_dilated.shape[2:], bf16),
            pltpu.VMEM(pool_weight.shape, bf16),
            pltpu.VMEM(proj_weight.shape, bf16),
            pltpu.VMEM((head_taps, LANES, width), bf16),
            pltpu.VMEM((cells + 2 * HEAD_REACH * cols, width), bf16),
            pltpu.VMEM((rows, cols), f32),
            pltpu.VMEM((2, rows, cols), f32),
            pltpu.VMEM((8, LANES), f32),
            pltpu.VMEM((8, LANES + channels), f32),
            pltpu.VMEM((8, LANES + channels), f32),
            pltpu.VMEM((8, channels), f32),
            pltpu.VMEM((8, channels), f32),
            pltpu.VMEM((8, LANES), f32),
            pltpu.VMEM((8, LANES), f32),
            pltpu.VMEM((8, LANES), f32),
            pltpu.VMEM((frame_count, 8, LANES), f32),
            pltpu.SemaphoreType.DMA((6,)),
            pltpu.SemaphoreType.DMA((8,)),
            pltpu.SemaphoreType.DMA((8,)),
            pltpu.SemaphoreType.DMA((frame_count - 1,)),
            pltpu.SemaphoreType.DMA((frame_count,)),
        ],
        compiler_params=pltpu.CompilerParams(
            collective_id=0, has_side_effects=True, vmem_limit_bytes=56 * 1024 * 1024
        ),
    )(
        x,
        clip_start,
        semantic,
        instance,
        jnp.asarray(place),
        aspp_point,
        aspp_dilated.reshape((taps,) + aspp_dilated.shape[2:]),
        pool_weight,
        proj_weight,
        head_weight,
        out_weight,
    )


def solution(mesh):
    placed = (
        P(("grp", "tm"), None, "row", None),
        P("grp"),
        P(("grp", "tm"), "row", None),
        P(("grp", "tm"), "row", None),
        P(),
        P(),
        P(),
        P(),
        P(),
        P(),
    )
    return jax.shard_map(
        shards,
        mesh=mesh,
        in_specs=placed,
        out_specs=(P(("grp", "tm"), None, "row", None), P("grp")),
        check_vma=False,
    )
```

```python
import functools

import jax
import jax.numpy as jnp
import numpy as np
from jax import lax
from jax.experimental import pallas as pl
from jax.experimental.pallas import tpu as pltpu
from jax.sharding import PartitionSpec as P

THING_FIRST = 11
DILATIONS = (6, 12, 18)
REACH = 18
EARLY = 20
HEAD_REACH = 2
LANES = 128
center_sigma = 8.0
offset_weight = 0.01
MESH = pl.DeviceIdType.MESH


def dot_nt(a, b):
    return lax.dot_general(a, b, (((1,), (1,)), ((), ())), preferred_element_type=jnp.float32)


def dot_nn(a, b):
    return lax.dot_general(a, b, (((1,), (0,)), ((), ())), preferred_element_type=jnp.float32)


def kernel(
    frame_count,
    rows,
    cols,
    tile_rows,
    x_ref,
    clip_ref,
    semantic_ref,
    instance_ref,
    place_ref,
    point_hbm,
    dilated_hbm,
    pool_hbm,
    proj_hbm,
    head_hbm,
    out_w_ref,
    pred_ref,
    losses_ref,
    own,
    nxt,
    acc,
    point_w,
    dilated_w,
    pool_w,
    proj_w,
    head_w,
    projected,
    heat_map,
    aim_map,
    out_full,
    small,
    small_in,
    total,
    total_in,
    err,
    err_all,
    local_sem,
    send_sem,
    recv_sem,
    all_send_sem,
    all_recv_sem,
):
    g = lax.axis_index("grp")
    t = lax.axis_index("tm")
    r = lax.axis_index("row")
    prev = lax.rem(t + frame_count - 1, frame_count)
    later = lax.rem(t + 1, frame_count)
    sister = 1 - r
    cells = rows * cols
    tile = tile_rows * cols
    tiles = rows // tile_rows
    first = REACH * cols
    channels = x_ref.shape[1]
    rim = REACH * cols
    early = EARLY * cols
    rest = cells - early

    def local(index, src, dst):
        return pltpu.make_async_copy(src, dst, local_sem.at[index])

    copies = [
        local(0, x_ref, own.at[pl.ds(first, cells)]),
        local(1, dilated_hbm, dilated_w),
        local(2, point_hbm, point_w),
        local(3, pool_hbm, pool_w),
        local(4, proj_hbm, proj_w),
        local(5, head_hbm, head_w.at[:, pl.ds(0, head_hbm.shape[1])]),
    ]
    for copy in copies:
        copy.start()

    barrier = pltpu.get_barrier_semaphore()
    bands = 2 * frame_count
    mine = 2 * t + r
    slots = [lax.rem(mine + step, bands) for step in range(1, bands)]
    for slot in slots:
        pl.semaphore_signal(
            barrier, inc=1, device_id=(g, slot // 2, slot % 2), device_id_type=MESH
        )
    pl.semaphore_wait(barrier, bands - 1)

    def remote(index, src, dst, device):
        return pltpu.make_async_remote_copy(
            src_ref=src,
            dst_ref=dst,
            send_sem=send_sem.at[index],
            recv_sem=recv_sem.at[index],
            device_id=device,
            device_id_type=MESH,
        )

    rim_start = pl.multiple_of((rows - REACH) * cols * (1 - r), 16)
    early_start = pl.multiple_of((cells - early) * (1 - r), 16)
    rest_start = pl.multiple_of(early * r, 16)
    early_mine = pl.multiple_of(first + early_start, 16)
    halo_there = pl.multiple_of((REACH + rows) * cols * r, 16)
    halo_zero = pl.multiple_of((REACH + rows) * cols * r, 16)
    rim_mine = pl.multiple_of(first + rim_start, 16)
    rest_mine = pl.multiple_of(first + rest_start, 16)

    own_halo = remote(
        0, x_ref.at[pl.ds(rim_start, rim)], own.at[pl.ds(halo_there, rim)], (g, t, sister)
    )
    next_early = remote(
        1, x_ref.at[pl.ds(early_start, early)], nxt.at[pl.ds(early_mine, early)], (g, prev, r)
    )
    next_rest = remote(
        2, x_ref.at[pl.ds(rest_start, rest)], nxt.at[pl.ds(rest_mine, rest)], (g, prev, r)
    )
    next_halo = remote(
        3, nxt.at[pl.ds(rim_mine, rim)], nxt.at[pl.ds(halo_there, rim)], (g, t, sister)
    )
    own_halo.start()
    next_early.start()
    next_rest.start()

    own[pl.ds(halo_zero, rim), :] = jnp.zeros((rim, channels), own.dtype)
    nxt[pl.ds(halo_zero, rim), :] = jnp.zeros((rim, channels), nxt.dtype)
    edge = HEAD_REACH * cols
    edge_zero = pl.multiple_of((HEAD_REACH + rows) * cols * r, 16)
    projected[pl.ds(edge_zero, edge), :] = jnp.zeros((edge, channels), projected.dtype)
    head_taps, head_width = head_hbm.shape[0], head_hbm.shape[1]
    head_w[:, pl.ds(head_width, LANES - head_width), :] = jnp.zeros(
        (head_taps, LANES - head_width, channels), head_w.dtype
    )

    label = jnp.where(semantic_ref[0] >= THING_FIRST, instance_ref[0], 0)
    flat = jnp.concatenate([label[y : y + 1] for y in range(rows)], axis=1)
    ids = lax.broadcasted_iota(jnp.int32, (LANES, cells), 0)
    onehot = jnp.where((ids == flat) & (flat > 0), 1.0, 0.0).astype(jnp.bfloat16)
    band_top = (r * rows).astype(jnp.float32)
    kind = lax.broadcasted_iota(jnp.int32, (8, cells), 0)
    place = place_ref[...] + jnp.where(kind == 1, band_top, 0.0)
    stats = dot_nt(place.astype(jnp.bfloat16), onehot)
    copies[0].wait()
    ones = jnp.ones((8, cells), jnp.bfloat16)
    channel_sums = dot_nn(ones, own[pl.ds(first, cells), :])
    small[:, :LANES] = stats
    small[:, LANES:] = channel_sums
    swap = remote(4, small, small_in, (g, t, sister))
    swap.start()
    swap.wait()
    total[...] = small[:, LANES:] + small_in[:, LANES:]
    frame_total = remote(5, total, total_in, (g, prev, r))
    frame_total.start()
    full_stats = small[:, :LANES] + small_in[:, :LANES]
    means = full_stats / jnp.maximum(full_stats[0:1], 1.0)
    high = means.astype(jnp.bfloat16)
    left = means - high.astype(jnp.float32)
    middle = left.astype(jnp.bfloat16)
    low = (left - middle.astype(jnp.float32)).astype(jnp.bfloat16)
    parts = jnp.concatenate([high, middle, low], axis=0)
    centre = dot_nn(parts, onehot)
    aim = centre[0:8] + (centre[8:16] + centre[16:24]) - place
    for axis in range(2):
        aim_map[axis] = jnp.concatenate(
            [aim[axis + 1 : axis + 2, y * cols : (y + 1) * cols] for y in range(rows)], axis=0
        )
    counted = label > 0
    square = aim_map[0] * aim_map[0] + aim_map[1] * aim_map[1]
    heat_map[...] = jnp.where(
        counted, jnp.exp(-square / (2.0 * center_sigma * center_sigma)), 0.0
    )

    part = out_w_ref.shape[1]
    out_full[...] = jnp.zeros(out_full.shape, jnp.float32)
    plain = out_w_ref[...].astype(jnp.float32)
    wide = jnp.concatenate([plain] * (LANES // part), axis=1)
    channel = lax.broadcasted_iota(jnp.int32, wide.shape, 0)
    group = lax.broadcasted_iota(jnp.int32, wide.shape, 1) // part
    out_full[pl.ds(0, 4), :] = jnp.where(group == (channel + 1) // 2, wide, 0.0)

    for copy in copies[1:]:
        copy.wait()

    col = lax.broadcasted_iota(jnp.int32, (tile_rows, cols, LANES), 1).reshape(tile, LANES)

    def widened(mask, width):
        return jnp.concatenate([mask] * (width // LANES), axis=1)

    def moved(value, step):
        width = value.shape[1]
        turned = pltpu.roll(value, (-step) % tile, 0)
        if step > 0:
            keep = col < cols - step
        else:
            keep = col >= -step
        return jnp.where(widened(keep, width), turned, 0.0)

    inner = 1 - 2 * r
    outer_half = r * (tiles - 1)
    inner_half = (1 - r) * (tiles - 1)

    def branch_sums(source, half, part, plan, with_point):
        lanes = pl.ds(part * channels, channels)
        base = first + half * tile
        results = [None]
        if with_point:
            rows_here = source[pl.ds(pl.multiple_of(base, 16), tile), :]
            results = [dot_nt(rows_here, point_w[:, lanes])]
        for b, spread in enumerate(DILATIONS):
            if not plan[b]:
                results.append(None)
                continue
            window = jnp.concatenate(
                [
                    source[pl.ds(pl.multiple_of(base + inner * (e * spread * cols), 16), tile), :]
                    for e in plan[b]
                ],
                axis=1,
            )
            value = None
            for j in (0, -1, 1):
                taps = jnp.concatenate(
                    [dilated_w[9 * b + 3 * (1 + inner * e) + j + 1, :, lanes] for e in plan[b]],
                    axis=1,
                )
                piece = dot_nt(window, taps)
                if j != 0:
                    piece = moved(piece, j * spread)
                value = piece if value is None else value + piece
            results.append(value)
        return results

    def cells_of(half):
        return pl.ds(pl.multiple_of(half * tile, 16), tile)

    def gather_sums(source, half, part, plan, with_point, fresh):
        for b, value in enumerate(branch_sums(source, half, part, plan, with_point)):
            if value is None:
                continue
            if fresh:
                acc[b, cells_of(half), :] = value
            else:
                acc[b, cells_of(half), :] += value

    every = (-1, 0, 1)
    own_halo.wait()
    gather_sums(own, inner_half, 0, (every, every, every), True, True)
    gather_sums(own, outer_half, 0, (every, every, (0, 1)), True, True)

    next_early.wait_recv()
    next_halo.start()

    frame_total.wait()
    clip_end = clip_ref[later] == 1
    later_total = jnp.where(clip_end, total[...], total_in[...])
    pooled = jnp.concatenate(
        [
            (total[...] / (2.0 * cells)).astype(jnp.bfloat16),
            (later_total / (2.0 * cells)).astype(jnp.bfloat16),
        ],
        axis=1,
    )
    feature = jnp.maximum(dot_nt(pooled, pool_w[...]), 0.0).astype(jnp.bfloat16)
    width = point_w.shape[0]
    bias = dot_nt(feature, proj_w[:, pl.ds(4 * width, width)])[0:1]

    def choose(start, count):
        @pl.loop(0, count // 2)
        def _(k):
            spot = pl.ds(pl.multiple_of(start + k * 2 * cols, 16), 2 * cols)
            nxt[spot, :] = jnp.where(clip_end, own[spot, :], nxt[spot, :])

    next_early.wait_send()
    next_halo.wait()
    choose(early_mine, EARLY)
    choose(pl.multiple_of((REACH + rows) * cols * (1 - r), 16), REACH)
    gather_sums(nxt, inner_half, 1, ((0, 1), (0, 1), (0, 1)), True, False)
    gather_sums(nxt, outer_half, 1, ((), (1,), (1,)), False, False)
    next_rest.wait()
    choose(rest_mine, rows - EARLY)

    edge_src = pl.multiple_of((HEAD_REACH + (rows - HEAD_REACH) * (1 - r)) * cols, 16)
    edge_dst = pl.multiple_of((HEAD_REACH + rows) * cols * r, 16)
    edge_copy = remote(
        6,
        projected.at[pl.ds(edge_src, edge)],
        projected.at[pl.ds(edge_dst, edge)],
        (g, t, sister),
    )

    def project(half, plan, with_point):
        mixed = bias
        for b, value in enumerate(branch_sums(nxt, half, 1, plan, with_point)):
            full = acc[b, cells_of(half), :]
            if value is not None:
                full = full + value
            branch = jnp.maximum(full, 0.0).astype(jnp.bfloat16)
            mixed = mixed + dot_nt(branch, proj_w[:, pl.ds(b * width, width)])
        spot = pl.ds(pl.multiple_of(HEAD_REACH * cols + half * tile, 16), tile)
        projected[spot, :] = jnp.maximum(mixed, 0.0).astype(jnp.bfloat16)

    project(inner_half, ((-1,), (-1,), (-1,)), False)
    edge_copy.start()
    project(outer_half, (every, (-1, 0), (0,)), True)

    size = 2 * HEAD_REACH + 1

    def head_tile(k):
        base = HEAD_REACH * cols + k * tile
        window = jnp.concatenate(
            [
                projected[pl.ds(pl.multiple_of(base + (i - HEAD_REACH) * cols, 16), tile), :]
                for i in range(size)
            ],
            axis=1,
        )
        value = None
        for j in range(size):
            taps = jnp.concatenate([head_w[size * i + j] for i in range(size)], axis=1)
            piece = dot_nt(window, taps)
            if j != HEAD_REACH:
                piece = moved(piece, j - HEAD_REACH)
            value = piece if value is None else value + piece
        head = jnp.maximum(value, 0.0).astype(jnp.bfloat16)
        weights = out_full[...].astype(jnp.bfloat16)
        maps = [
            dot_nt(weights, head[y * cols : (y + 1) * cols]) for y in range(tile_rows)
        ]
        for c in range(4):
            pred_ref[0, c, pl.ds(pl.multiple_of(k * tile_rows, 8), tile_rows), :] = (
                jnp.concatenate([value[c : c + 1] for value in maps], axis=0)
            )

    head_tile(outer_half)
    edge_copy.wait()
    head_tile(inner_half)

    gap = pred_ref[0, 0] - heat_map[...]
    offset_gap = jnp.abs(pred_ref[0, 1] - aim_map[0]) + jnp.abs(pred_ref[0, 2] - aim_map[1])
    err[...] = jnp.zeros(err.shape, jnp.float32)
    err[0:1, pl.ds(0, cols)] = jnp.sum(gap * gap, axis=0, keepdims=True)
    err[1:2, pl.ds(0, cols)] = jnp.sum(
        jnp.where(counted, offset_gap, 0.0), axis=0, keepdims=True
    )
    err[2:3, pl.ds(0, cols)] = jnp.sum(jnp.where(counted, 1.0, 0.0), axis=0, keepdims=True)
    err_all[mine] = err[...]

    def spread_copy(step, slot):
        return pltpu.make_async_remote_copy(
            src_ref=err,
            dst_ref=err_all.at[slot],
            send_sem=all_send_sem.at[step],
            recv_sem=all_recv_sem.at[slot],
            device_id=(g, slots[step] // 2, slots[step] % 2),
            device_id_type=MESH,
        )

    for step in range(bands - 1):
        spread_copy(step, mine).start()
    for step in range(bands - 1):
        spread_copy(step, mine).wait_send()
        spread_copy(step, slots[step]).wait_recv()
    summed = err_all[0]
    for slot in range(1, bands):
        summed = summed + err_all[slot]
    sums = jnp.sum(summed, axis=1, keepdims=True)
    center_loss = sums[0:1] / (frame_count * 2 * cells)
    offset_loss = offset_weight * sums[1:2] / jnp.maximum(sums[2:3], 1.0)
    losses_ref[0] = center_loss[0, 0]
    losses_ref[1] = offset_loss[0, 0]


def shards(
    frames,
    clip_start,
    semantic,
    instance,
    aspp_point,
    aspp_dilated,
    pool_weight,
    proj_weight,
    head_weight,
    out_weight,
):
    _, channels, rows, cols = frames.shape
    cells = rows * cols
    frame_count = clip_start.shape[0]
    width = aspp_point.shape[0]
    tile_rows = rows // 2
    place = np.zeros((8, cells), np.float32)
    place[0] = 1.0
    place[1] = np.arange(cells) // cols
    place[2] = np.arange(cells) % cols
    x = frames[0].reshape(channels, cells).T
    vmem = pl.BlockSpec(memory_space=pltpu.VMEM)
    anywhere = pl.BlockSpec(memory_space=pl.ANY)
    taps = aspp_dilated.shape[0] * aspp_dilated.shape[1]
    head_taps = head_weight.shape[0]
    tall = cells + 2 * REACH * cols
    bf16, f32 = jnp.bfloat16, jnp.float32
    return pl.pallas_call(
        functools.partial(kernel, frame_count, rows, cols, tile_rows),
        out_shape=(
            jax.ShapeDtypeStruct((1, 4, rows, cols), f32),
            jax.ShapeDtypeStruct((2,), f32),
        ),
        in_specs=[
            anywhere,
            pl.BlockSpec(memory_space=pltpu.SMEM),
            vmem,
            vmem,
            vmem,
            anywhere,
            anywhere,
            anywhere,
            anywhere,
            anywhere,
            vmem,
        ],
        out_specs=(vmem, pl.BlockSpec(memory_space=pltpu.SMEM)),
        scratch_shapes=[
            pltpu.VMEM((tall, channels), bf16),
            pltpu.VMEM((tall, channels), bf16),
            pltpu.VMEM((4, cells, width), f32),
            pltpu.VMEM(aspp_point.shape, bf16),
            pltpu.VMEM((taps,) + aspp_dilated.shape[2:], bf16),
            pltpu.VMEM(pool_weight.shape, bf16),
            pltpu.VMEM(proj_weight.shape, bf16),
            pltpu.VMEM((head_taps, LANES, width), bf16),
            pltpu.VMEM((cells + 2 * HEAD_REACH * cols, width), bf16),
            pltpu.VMEM((rows, cols), f32),
            pltpu.VMEM((2, rows, cols), f32),
            pltpu.VMEM((8, LANES), f32),
            pltpu.VMEM((8, LANES + channels), f32),
            pltpu.VMEM((8, LANES + channels), f32),
            pltpu.VMEM((8, channels), f32),
            pltpu.VMEM((8, channels), f32),
            pltpu.VMEM((8, LANES), f32),
            pltpu.VMEM((2 * frame_count, 8, LANES), f32),
            pltpu.SemaphoreType.DMA((6,)),
            pltpu.SemaphoreType.DMA((7,)),
            pltpu.SemaphoreType.DMA((7,)),
            pltpu.SemaphoreType.DMA((2 * frame_count - 1,)),
            pltpu.SemaphoreType.DMA((2 * frame_count,)),
        ],
        compiler_params=pltpu.CompilerParams(
            collective_id=0, has_side_effects=True, vmem_limit_bytes=56 * 1024 * 1024
        ),
    )(
        x,
        clip_start,
        semantic,
        instance,
        jnp.asarray(place),
        aspp_point,
        aspp_dilated.reshape((taps,) + aspp_dilated.shape[2:]),
        pool_weight,
        proj_weight,
        head_weight,
        out_weight,
    )


def solution(mesh):
    placed = (
        P(("grp", "tm"), None, "row", None),
        P("grp"),
        P(("grp", "tm"), "row", None),
        P(("grp", "tm"), "row", None),
        P(),
        P(),
        P(),
        P(),
        P(),
        P(),
    )
    return jax.shard_map(
        shards,
        mesh=mesh,
        in_specs=placed,
        out_specs=(P(("grp", "tm"), None, "row", None), P("grp")),
        check_vma=False,
    )
```

```python
import functools

import jax
import jax.numpy as jnp
import numpy as np
from jax import lax
from jax.experimental import pallas as pl
from jax.experimental.pallas import tpu as pltpu
from jax.sharding import PartitionSpec as P

THING_FIRST = 11
DILATIONS = (6, 12, 18)
REACH = 18
EARLY = 20
HEAD_REACH = 2
LANES = 128
center_sigma = 8.0
offset_weight = 0.01
MESH = pl.DeviceIdType.MESH


def dot_nt(a, b):
    return lax.dot_general(a, b, (((1,), (1,)), ((), ())), preferred_element_type=jnp.float32)


def dot_nn(a, b):
    return lax.dot_general(a, b, (((1,), (0,)), ((), ())), preferred_element_type=jnp.float32)


def kernel(
    frame_count,
    rows,
    cols,
    tile_rows,
    x_ref,
    clip_ref,
    semantic_ref,
    instance_ref,
    place_ref,
    point_hbm,
    dilated_hbm,
    pool_hbm,
    proj_hbm,
    head_hbm,
    out_w_ref,
    pred_ref,
    losses_ref,
    own,
    nxt,
    acc,
    point_w,
    dilated_w,
    pool_w,
    proj_w,
    head_w,
    projected,
    heat_map,
    aim_map,
    out_full,
    small,
    small_in,
    total,
    total_in,
    err,
    err_all,
    local_sem,
    send_sem,
    recv_sem,
    all_send_sem,
    all_recv_sem,
):
    g = lax.axis_index("grp")
    t = lax.axis_index("tm")
    r = lax.axis_index("row")
    prev = lax.rem(t + frame_count - 1, frame_count)
    later = lax.rem(t + 1, frame_count)
    sister = 1 - r
    cells = rows * cols
    tile = tile_rows * cols
    tiles = rows // tile_rows
    first = REACH * cols
    channels = x_ref.shape[1]
    rim = REACH * cols
    early = EARLY * cols
    rest = cells - early

    def local(index, src, dst):
        return pltpu.make_async_copy(src, dst, local_sem.at[index])

    copies = [
        local(0, x_ref, own.at[pl.ds(first, cells)]),
        local(1, dilated_hbm, dilated_w),
        local(2, point_hbm, point_w),
        local(3, pool_hbm, pool_w),
        local(4, proj_hbm, proj_w),
        local(5, head_hbm, head_w.at[:, pl.ds(0, head_hbm.shape[1])]),
    ]
    for copy in copies:
        copy.start()

    barrier = pltpu.get_barrier_semaphore()
    bands = 2 * frame_count
    mine = 2 * t + r
    slots = [lax.rem(mine + step, bands) for step in range(1, bands)]
    for slot in slots:
        pl.semaphore_signal(
            barrier, inc=1, device_id=(g, slot // 2, slot % 2), device_id_type=MESH
        )
    pl.semaphore_wait(barrier, bands - 1)

    def remote(index, src, dst, device):
        return pltpu.make_async_remote_copy(
            src_ref=src,
            dst_ref=dst,
            send_sem=send_sem.at[index],
            recv_sem=recv_sem.at[index],
            device_id=device,
            device_id_type=MESH,
        )

    rim_start = pl.multiple_of((rows - REACH) * cols * (1 - r), 16)
    early_start = pl.multiple_of((cells - early) * (1 - r), 16)
    rest_start = pl.multiple_of(early * r, 16)
    early_mine = pl.multiple_of(first + early_start, 16)
    halo_there = pl.multiple_of((REACH + rows) * cols * r, 16)
    halo_zero = pl.multiple_of((REACH + rows) * cols * r, 16)
    rim_mine = pl.multiple_of(first + rim_start, 16)
    rest_mine = pl.multiple_of(first + rest_start, 16)

    own_halo = remote(
        0, x_ref.at[pl.ds(rim_start, rim)], own.at[pl.ds(halo_there, rim)], (g, t, sister)
    )
    next_early = remote(
        1, x_ref.at[pl.ds(early_start, early)], nxt.at[pl.ds(early_mine, early)], (g, prev, r)
    )
    next_rest = remote(
        2, x_ref.at[pl.ds(rest_start, rest)], nxt.at[pl.ds(rest_mine, rest)], (g, prev, r)
    )
    next_halo = remote(
        3, nxt.at[pl.ds(rim_mine, rim)], nxt.at[pl.ds(halo_there, rim)], (g, t, sister)
    )
    own_halo.start()
    next_early.start()
    next_rest.start()

    own[pl.ds(halo_zero, rim), :] = jnp.zeros((rim, channels), own.dtype)
    nxt[pl.ds(halo_zero, rim), :] = jnp.zeros((rim, channels), nxt.dtype)
    edge = HEAD_REACH * cols
    edge_zero = pl.multiple_of((HEAD_REACH + rows) * cols * r, 16)
    projected[pl.ds(edge_zero, edge), :] = jnp.zeros((edge, channels), projected.dtype)
    head_taps, head_width = head_hbm.shape[0], head_hbm.shape[1]
    head_w[:, pl.ds(head_width, LANES - head_width), :] = jnp.zeros(
        (head_taps, LANES - head_width, channels), head_w.dtype
    )

    label = jnp.where(semantic_ref[0] >= THING_FIRST, instance_ref[0], 0)
    flat = jnp.concatenate([label[y : y + 1] for y in range(rows)], axis=1)
    ids = lax.broadcasted_iota(jnp.int32, (LANES, cells), 0)
    onehot = jnp.where((ids == flat) & (flat > 0), 1.0, 0.0).astype(jnp.bfloat16)
    band_top = (r * rows).astype(jnp.float32)
    kind = lax.broadcasted_iota(jnp.int32, (8, cells), 0)
    place = place_ref[...] + jnp.where(kind == 1, band_top, 0.0)
    stats = dot_nt(place.astype(jnp.bfloat16), onehot)
    copies[0].wait()
    ones = jnp.ones((8, cells), jnp.bfloat16)
    channel_sums = dot_nn(ones, own[pl.ds(first, cells), :])
    small[:, :LANES] = stats
    small[:, LANES:] = channel_sums
    swap = remote(4, small, small_in, (g, t, sister))
    swap.start()
    swap.wait()
    total[...] = small[:, LANES:] + small_in[:, LANES:]
    frame_total = remote(5, total, total_in, (g, prev, r))
    frame_total.start()
    full_stats = small[:, :LANES] + small_in[:, :LANES]
    means = full_stats / jnp.maximum(full_stats[0:1], 1.0)
    high = means.astype(jnp.bfloat16)
    left = means - high.astype(jnp.float32)
    middle = left.astype(jnp.bfloat16)
    low = (left - middle.astype(jnp.float32)).astype(jnp.bfloat16)
    parts = jnp.concatenate([high, middle, low], axis=0)
    centre = dot_nn(parts, onehot)
    aim = centre[0:8] + (centre[8:16] + centre[16:24]) - place
    for axis in range(2):
        aim_map[axis] = jnp.concatenate(
            [aim[axis + 1 : axis + 2, y * cols : (y + 1) * cols] for y in range(rows)], axis=0
        )
    counted = label > 0
    square = aim_map[0] * aim_map[0] + aim_map[1] * aim_map[1]
    heat_map[...] = jnp.where(
        counted, jnp.exp(-square / (2.0 * center_sigma * center_sigma)), 0.0
    )

    part = out_w_ref.shape[1]
    out_full[...] = jnp.zeros(out_full.shape, jnp.float32)
    plain = out_w_ref[...].astype(jnp.float32)
    wide = jnp.concatenate([plain] * (LANES // part), axis=1)
    channel = lax.broadcasted_iota(jnp.int32, wide.shape, 0)
    group = lax.broadcasted_iota(jnp.int32, wide.shape, 1) // part
    out_full[pl.ds(0, 4), :] = jnp.where(group == (channel + 1) // 2, wide, 0.0)

    for copy in copies[1:]:
        copy.wait()

    def useful(step):
        low = max(step, 0) // 16 * 16
        high = -((-(cols + min(step, 0))) // 16) * 16
        return low, high

    def moved(value, step):
        if step == 0:
            return value
        low, high = useful(step)
        width = value.shape[1]
        lines = value.reshape(tile_rows, high - low, width)
        blank = jnp.zeros((tile_rows, abs(step), width), value.dtype)
        if step > 0:
            joined = [lines[:, step - low : cols - low], blank]
        else:
            joined = [blank, lines[:, : cols + step]]
        return jnp.concatenate(joined, axis=1).reshape(tile, width)

    inner = 1 - 2 * r
    outer_half = r * (tiles - 1)
    inner_half = (1 - r) * (tiles - 1)

    def branch_sums(source, half, part, plan, with_point):
        lanes = pl.ds(part * channels, channels)
        base = first + half * tile
        results = [None] * 10
        if with_point:
            rows_here = source[pl.ds(pl.multiple_of(base, 16), tile), :]
            results[0] = dot_nt(rows_here, point_w[:, lanes])
        for b, spread in enumerate(DILATIONS):
            if not plan[b]:
                continue
            window = jnp.concatenate(
                [
                    source[pl.ds(pl.multiple_of(base + inner * (e * spread * cols), 16), tile), :]
                    for e in plan[b]
                ],
                axis=1,
            )
            lines = window.reshape(tile_rows, cols, window.shape[1])
            for j in (-1, 0, 1):
                taps = jnp.concatenate(
                    [dilated_w[9 * b + 3 * (1 + inner * e) + j + 1, :, lanes] for e in plan[b]],
                    axis=1,
                )
                low, high = useful(j * spread)
                part_lines = lines[:, low:high].reshape(-1, window.shape[1])
                results[3 * b + j + 2] = dot_nt(part_lines, taps)
        return results

    def spot_of(slot, half):
        lateral = (slot - 1) % 3 - 1 if slot else 0
        low, high = useful(lateral * DILATIONS[(slot - 1) // 3] if slot else 0)
        return pl.ds(pl.multiple_of(half * tile, 16), tile_rows * (high - low))

    def gather_sums(source, half, part, plan, with_point, fresh):
        for slot, value in enumerate(branch_sums(source, half, part, plan, with_point)):
            if value is None:
                continue
            if fresh:
                acc[slot, spot_of(slot, half), :] = value
            else:
                acc[slot, spot_of(slot, half), :] += value

    every = (-1, 0, 1)
    own_halo.wait()
    gather_sums(own, inner_half, 0, (every, every, every), True, True)
    gather_sums(own, outer_half, 0, (every, every, (0, 1)), True, True)

    next_early.wait_recv()
    next_halo.start()

    frame_total.wait()
    clip_end = clip_ref[later] == 1
    later_total = jnp.where(clip_end, total[...], total_in[...])
    pooled = jnp.concatenate(
        [
            (total[...] / (2.0 * cells)).astype(jnp.bfloat16),
            (later_total / (2.0 * cells)).astype(jnp.bfloat16),
        ],
        axis=1,
    )
    feature = jnp.maximum(dot_nt(pooled, pool_w[...]), 0.0).astype(jnp.bfloat16)
    width = point_w.shape[0]
    bias = dot_nt(feature, proj_w[:, pl.ds(4 * width, width)])[0:1]

    def choose(start, count):
        @pl.loop(0, count // 2)
        def _(k):
            spot = pl.ds(pl.multiple_of(start + k * 2 * cols, 16), 2 * cols)
            nxt[spot, :] = jnp.where(clip_end, own[spot, :], nxt[spot, :])

    next_early.wait_send()
    next_halo.wait()
    choose(early_mine, EARLY)
    choose(pl.multiple_of((REACH + rows) * cols * (1 - r), 16), REACH)
    gather_sums(nxt, inner_half, 1, ((0, 1), (0, 1), (0, 1)), True, False)
    gather_sums(nxt, outer_half, 1, ((), (1,), (1,)), False, False)
    next_rest.wait()
    choose(rest_mine, rows - EARLY)

    edge_src = pl.multiple_of((HEAD_REACH + (rows - HEAD_REACH) * (1 - r)) * cols, 16)
    edge_dst = pl.multiple_of((HEAD_REACH + rows) * cols * r, 16)
    edge_copy = remote(
        6,
        projected.at[pl.ds(edge_src, edge)],
        projected.at[pl.ds(edge_dst, edge)],
        (g, t, sister),
    )

    def project(half, plan, with_point):
        sums = []
        for slot, value in enumerate(branch_sums(nxt, half, 1, plan, with_point)):
            full = acc[slot, spot_of(slot, half), :]
            sums.append(full if value is None else full + value)
        mixed = bias
        for b in range(4):
            if b == 0:
                full = sums[0]
            else:
                spread = DILATIONS[b - 1]
                full = (
                    sums[3 * b - 1]
                    + moved(sums[3 * b - 2], -spread)
                    + moved(sums[3 * b], spread)
                )
            branch = jnp.maximum(full, 0.0).astype(jnp.bfloat16)
            mixed = mixed + dot_nt(branch, proj_w[:, pl.ds(b * width, width)])
        spot = pl.ds(pl.multiple_of(HEAD_REACH * cols + half * tile, 16), tile)
        projected[spot, :] = jnp.maximum(mixed, 0.0).astype(jnp.bfloat16)

    project(inner_half, ((-1,), (-1,), (-1,)), False)
    edge_copy.start()
    project(outer_half, (every, (-1, 0), (0,)), True)

    size = 2 * HEAD_REACH + 1

    def head_tile(k):
        base = HEAD_REACH * cols + k * tile
        window = jnp.concatenate(
            [
                projected[pl.ds(pl.multiple_of(base + (i - HEAD_REACH) * cols, 16), tile), :]
                for i in range(size)
            ],
            axis=1,
        )
        value = None
        for j in range(size):
            taps = jnp.concatenate([head_w[size * i + j] for i in range(size)], axis=1)
            piece = dot_nt(window, taps)
            if j != HEAD_REACH:
                piece = moved(piece, j - HEAD_REACH)
            value = piece if value is None else value + piece
        head = jnp.maximum(value, 0.0).astype(jnp.bfloat16)
        weights = out_full[...].astype(jnp.bfloat16)
        maps = [
            dot_nt(weights, head[y * cols : (y + 1) * cols]) for y in range(tile_rows)
        ]
        for c in range(4):
            pred_ref[0, c, pl.ds(pl.multiple_of(k * tile_rows, 8), tile_rows), :] = (
                jnp.concatenate([value[c : c + 1] for value in maps], axis=0)
            )

    head_tile(outer_half)
    edge_copy.wait()
    head_tile(inner_half)

    gap = pred_ref[0, 0] - heat_map[...]
    offset_gap = jnp.abs(pred_ref[0, 1] - aim_map[0]) + jnp.abs(pred_ref[0, 2] - aim_map[1])
    err[...] = jnp.zeros(err.shape, jnp.float32)
    err[0:1, pl.ds(0, cols)] = jnp.sum(gap * gap, axis=0, keepdims=True)
    err[1:2, pl.ds(0, cols)] = jnp.sum(
        jnp.where(counted, offset_gap, 0.0), axis=0, keepdims=True
    )
    err[2:3, pl.ds(0, cols)] = jnp.sum(jnp.where(counted, 1.0, 0.0), axis=0, keepdims=True)
    err_all[mine] = err[...]

    def spread_copy(step, slot):
        return pltpu.make_async_remote_copy(
            src_ref=err,
            dst_ref=err_all.at[slot],
            send_sem=all_send_sem.at[step],
            recv_sem=all_recv_sem.at[slot],
            device_id=(g, slots[step] // 2, slots[step] % 2),
            device_id_type=MESH,
        )

    for step in range(bands - 1):
        spread_copy(step, mine).start()
    for step in range(bands - 1):
        spread_copy(step, mine).wait_send()
        spread_copy(step, slots[step]).wait_recv()
    summed = err_all[0]
    for slot in range(1, bands):
        summed = summed + err_all[slot]
    sums = jnp.sum(summed, axis=1, keepdims=True)
    center_loss = sums[0:1] / (frame_count * 2 * cells)
    offset_loss = offset_weight * sums[1:2] / jnp.maximum(sums[2:3], 1.0)
    losses_ref[0] = center_loss[0, 0]
    losses_ref[1] = offset_loss[0, 0]


def shards(
    frames,
    clip_start,
    semantic,
    instance,
    aspp_point,
    aspp_dilated,
    pool_weight,
    proj_weight,
    head_weight,
    out_weight,
):
    _, channels, rows, cols = frames.shape
    cells = rows * cols
    frame_count = clip_start.shape[0]
    width = aspp_point.shape[0]
    tile_rows = rows // 2
    place = np.zeros((8, cells), np.float32)
    place[0] = 1.0
    place[1] = np.arange(cells) // cols
    place[2] = np.arange(cells) % cols
    x = frames[0].reshape(channels, cells).T
    vmem = pl.BlockSpec(memory_space=pltpu.VMEM)
    anywhere = pl.BlockSpec(memory_space=pl.ANY)
    taps = aspp_dilated.shape[0] * aspp_dilated.shape[1]
    head_taps = head_weight.shape[0]
    tall = cells + 2 * REACH * cols
    bf16, f32 = jnp.bfloat16, jnp.float32
    return pl.pallas_call(
        functools.partial(kernel, frame_count, rows, cols, tile_rows),
        out_shape=(
            jax.ShapeDtypeStruct((1, 4, rows, cols), f32),
            jax.ShapeDtypeStruct((2,), f32),
        ),
        in_specs=[
            anywhere,
            pl.BlockSpec(memory_space=pltpu.SMEM),
            vmem,
            vmem,
            vmem,
            anywhere,
            anywhere,
            anywhere,
            anywhere,
            anywhere,
            vmem,
        ],
        out_specs=(vmem, pl.BlockSpec(memory_space=pltpu.SMEM)),
        scratch_shapes=[
            pltpu.VMEM((tall, channels), bf16),
            pltpu.VMEM((tall, channels), bf16),
            pltpu.VMEM((10, cells, width), f32),
            pltpu.VMEM(aspp_point.shape, bf16),
            pltpu.VMEM((taps,) + aspp_dilated.shape[2:], bf16),
            pltpu.VMEM(pool_weight.shape, bf16),
            pltpu.VMEM(proj_weight.shape, bf16),
            pltpu.VMEM((head_taps, LANES, width), bf16),
            pltpu.VMEM((cells + 2 * HEAD_REACH * cols, width), bf16),
            pltpu.VMEM((rows, cols), f32),
            pltpu.VMEM((2, rows, cols), f32),
            pltpu.VMEM((8, LANES), f32),
            pltpu.VMEM((8, LANES + channels), f32),
            pltpu.VMEM((8, LANES + channels), f32),
            pltpu.VMEM((8, channels), f32),
            pltpu.VMEM((8, channels), f32),
            pltpu.VMEM((8, LANES), f32),
            pltpu.VMEM((2 * frame_count, 8, LANES), f32),
            pltpu.SemaphoreType.DMA((6,)),
            pltpu.SemaphoreType.DMA((7,)),
            pltpu.SemaphoreType.DMA((7,)),
            pltpu.SemaphoreType.DMA((2 * frame_count - 1,)),
            pltpu.SemaphoreType.DMA((2 * frame_count,)),
        ],
        compiler_params=pltpu.CompilerParams(
            collective_id=0, has_side_effects=True, vmem_limit_bytes=56 * 1024 * 1024
        ),
    )(
        x,
        clip_start,
        semantic,
        instance,
        jnp.asarray(place),
        aspp_point,
        aspp_dilated.reshape((taps,) + aspp_dilated.shape[2:]),
        pool_weight,
        proj_weight,
        head_weight,
        out_weight,
    )


def solution(mesh):
    placed = (
        P(("grp", "tm"), None, "row", None),
        P("grp"),
        P(("grp", "tm"), "row", None),
        P(("grp", "tm"), "row", None),
        P(),
        P(),
        P(),
        P(),
        P(),
        P(),
    )
    return jax.shard_map(
        shards,
        mesh=mesh,
        in_specs=placed,
        out_specs=(P(("grp", "tm"), None, "row", None), P("grp")),
        check_vma=False,
    )
```

```python
import functools

import jax
import jax.numpy as jnp
import numpy as np
from jax import lax
from jax.experimental import pallas as pl
from jax.experimental.pallas import tpu as pltpu
from jax.sharding import PartitionSpec as P

THING_FIRST = 11
DILATIONS = (6, 12, 18)
REACH = 18
EARLY = 20
HEAD_REACH = 2
LANES = 128
center_sigma = 8.0
offset_weight = 0.01
MESH = pl.DeviceIdType.MESH


def dot_nt(a, b):
    return lax.dot_general(a, b, (((1,), (1,)), ((), ())), preferred_element_type=jnp.float32)


def dot_nn(a, b):
    return lax.dot_general(a, b, (((1,), (0,)), ((), ())), preferred_element_type=jnp.float32)


def kernel(
    frame_count,
    rows,
    cols,
    tile_rows,
    x_ref,
    clip_ref,
    semantic_ref,
    instance_ref,
    place_ref,
    point_hbm,
    dilated_hbm,
    pool_hbm,
    proj_hbm,
    head_hbm,
    out_w_ref,
    pred_ref,
    losses_ref,
    own,
    nxt,
    acc,
    point_w,
    dilated_w,
    pool_w,
    proj_w,
    head_w,
    projected,
    heat_map,
    aim_map,
    out_full,
    small,
    small_in,
    total,
    total_in,
    err,
    err_all,
    local_sem,
    send_sem,
    recv_sem,
    all_send_sem,
    all_recv_sem,
):
    g = lax.axis_index("grp")
    t = lax.axis_index("tm")
    r = lax.axis_index("row")
    prev = lax.rem(t + frame_count - 1, frame_count)
    later = lax.rem(t + 1, frame_count)
    sister = 1 - r
    cells = rows * cols
    tile = tile_rows * cols
    tiles = rows // tile_rows
    first = REACH * cols
    channels = x_ref.shape[1]
    rim = REACH * cols
    early = EARLY * cols
    rest = cells - early

    def local(index, src, dst):
        return pltpu.make_async_copy(src, dst, local_sem.at[index])

    copies = [
        local(0, x_ref, own.at[pl.ds(first, cells)]),
        local(1, dilated_hbm, dilated_w),
        local(2, point_hbm, point_w),
        local(3, pool_hbm, pool_w),
        local(4, proj_hbm, proj_w),
        local(5, head_hbm, head_w.at[:, pl.ds(0, head_hbm.shape[1])]),
    ]
    for copy in copies:
        copy.start()

    barrier = pltpu.get_barrier_semaphore()
    bands = 2 * frame_count
    mine = 2 * t + r
    slots = [lax.rem(mine + step, bands) for step in range(1, bands)]
    for slot in slots:
        pl.semaphore_signal(
            barrier, inc=1, device_id=(g, slot // 2, slot % 2), device_id_type=MESH
        )
    pl.semaphore_wait(barrier, bands - 1)

    def remote(index, src, dst, device):
        return pltpu.make_async_remote_copy(
            src_ref=src,
            dst_ref=dst,
            send_sem=send_sem.at[index],
            recv_sem=recv_sem.at[index],
            device_id=device,
            device_id_type=MESH,
        )

    rim_start = pl.multiple_of((rows - REACH) * cols * (1 - r), 16)
    early_start = pl.multiple_of((cells - early) * (1 - r), 16)
    rest_start = pl.multiple_of(early * r, 16)
    early_mine = pl.multiple_of(first + early_start, 16)
    halo_there = pl.multiple_of((REACH + rows) * cols * r, 16)
    halo_zero = pl.multiple_of((REACH + rows) * cols * r, 16)
    rim_mine = pl.multiple_of(first + rim_start, 16)
    rest_mine = pl.multiple_of(first + rest_start, 16)

    own_halo = remote(
        0, x_ref.at[pl.ds(rim_start, rim)], own.at[pl.ds(halo_there, rim)], (g, t, sister)
    )
    next_early = remote(
        1, x_ref.at[pl.ds(early_start, early)], nxt.at[pl.ds(early_mine, early)], (g, prev, r)
    )
    next_rest = remote(
        2, x_ref.at[pl.ds(rest_start, rest)], nxt.at[pl.ds(rest_mine, rest)], (g, prev, r)
    )
    next_halo = remote(
        3, nxt.at[pl.ds(rim_mine, rim)], nxt.at[pl.ds(halo_there, rim)], (g, t, sister)
    )
    own_halo.start()
    next_early.start()

    own[pl.ds(halo_zero, rim), :] = jnp.zeros((rim, channels), own.dtype)
    nxt[pl.ds(halo_zero, rim), :] = jnp.zeros((rim, channels), nxt.dtype)
    edge = HEAD_REACH * cols
    edge_zero = pl.multiple_of((HEAD_REACH + rows) * cols * r, 16)
    projected[pl.ds(edge_zero, edge), :] = jnp.zeros((edge, channels), projected.dtype)
    head_taps, head_width = head_hbm.shape[0], head_hbm.shape[1]
    head_w[:, pl.ds(head_width, LANES - head_width), :] = jnp.zeros(
        (head_taps, LANES - head_width, channels), head_w.dtype
    )

    label = jnp.where(semantic_ref[0] >= THING_FIRST, instance_ref[0], 0)
    flat = jnp.concatenate([label[y : y + 1] for y in range(rows)], axis=1)
    ids = lax.broadcasted_iota(jnp.int32, (LANES, cells), 0)
    onehot = jnp.where((ids == flat) & (flat > 0), 1.0, 0.0).astype(jnp.bfloat16)
    band_top = (r * rows).astype(jnp.float32)
    kind = lax.broadcasted_iota(jnp.int32, (8, cells), 0)
    place = place_ref[...] + jnp.where(kind == 1, band_top, 0.0)
    stats = dot_nt(place.astype(jnp.bfloat16), onehot)
    copies[0].wait()
    ones = jnp.ones((8, cells), jnp.bfloat16)
    channel_sums = dot_nn(ones, own[pl.ds(first, cells), :])
    small[:, :LANES] = stats
    small[:, LANES:] = channel_sums
    swap = remote(4, small, small_in, (g, t, sister))
    swap.start()
    swap.wait()
    total[...] = small[:, LANES:] + small_in[:, LANES:]
    frame_total = remote(5, total, total_in, (g, prev, r))
    frame_total.start()
    full_stats = small[:, :LANES] + small_in[:, :LANES]
    means = full_stats / jnp.maximum(full_stats[0:1], 1.0)
    high = means.astype(jnp.bfloat16)
    left = means - high.astype(jnp.float32)
    middle = left.astype(jnp.bfloat16)
    low = (left - middle.astype(jnp.float32)).astype(jnp.bfloat16)
    parts = jnp.concatenate([high, middle, low], axis=0)
    centre = dot_nn(parts, onehot)
    aim = centre[0:8] + (centre[8:16] + centre[16:24]) - place
    for axis in range(2):
        aim_map[axis] = jnp.concatenate(
            [aim[axis + 1 : axis + 2, y * cols : (y + 1) * cols] for y in range(rows)], axis=0
        )
    counted = label > 0
    square = aim_map[0] * aim_map[0] + aim_map[1] * aim_map[1]
    heat_map[...] = jnp.where(
        counted, jnp.exp(-square / (2.0 * center_sigma * center_sigma)), 0.0
    )

    part = out_w_ref.shape[1]
    out_full[...] = jnp.zeros(out_full.shape, jnp.float32)
    plain = out_w_ref[...].astype(jnp.float32)
    wide = jnp.concatenate([plain] * (LANES // part), axis=1)
    channel = lax.broadcasted_iota(jnp.int32, wide.shape, 0)
    group = lax.broadcasted_iota(jnp.int32, wide.shape, 1) // part
    out_full[pl.ds(0, 4), :] = jnp.where(group == (channel + 1) // 2, wide, 0.0)

    for copy in copies[1:]:
        copy.wait()

    def useful(step):
        low = max(step, 0) // 16 * 16
        high = -((-(cols + min(step, 0))) // 16) * 16
        return low, high

    def moved(value, step):
        if step == 0:
            return value
        low, high = useful(step)
        width = value.shape[1]
        lines = value.reshape(tile_rows, high - low, width)
        blank = jnp.zeros((tile_rows, abs(step), width), value.dtype)
        if step > 0:
            joined = [lines[:, step - low : cols - low], blank]
        else:
            joined = [blank, lines[:, : cols + step]]
        return jnp.concatenate(joined, axis=1).reshape(tile, width)

    inner = 1 - 2 * r
    outer_half = r * (tiles - 1)
    inner_half = (1 - r) * (tiles - 1)

    def branch_sums(source, half, part, plan, with_point):
        lanes = pl.ds(part * channels, channels)
        base = first + half * tile
        results = [None] * 10
        if with_point:
            rows_here = source[pl.ds(pl.multiple_of(base, 16), tile), :]
            results[0] = dot_nt(rows_here, point_w[:, lanes])
        for b, spread in enumerate(DILATIONS):
            if not plan[b]:
                continue
            window = jnp.concatenate(
                [
                    source[pl.ds(pl.multiple_of(base + inner * (e * spread * cols), 16), tile), :]
                    for e in plan[b]
                ],
                axis=1,
            )
            lines = window.reshape(tile_rows, cols, window.shape[1])
            for j in (-1, 0, 1):
                taps = jnp.concatenate(
                    [dilated_w[9 * b + 3 * (1 + inner * e) + j + 1, :, lanes] for e in plan[b]],
                    axis=1,
                )
                low, high = useful(j * spread)
                part_lines = lines[:, low:high].reshape(-1, window.shape[1])
                results[3 * b + j + 2] = dot_nt(part_lines, taps)
        return results

    def spot_of(slot, half):
        lateral = (slot - 1) % 3 - 1 if slot else 0
        low, high = useful(lateral * DILATIONS[(slot - 1) // 3] if slot else 0)
        return pl.ds(pl.multiple_of(half * tile, 16), tile_rows * (high - low))

    def gather_sums(source, half, part, plan, with_point, fresh):
        for slot, value in enumerate(branch_sums(source, half, part, plan, with_point)):
            if value is None:
                continue
            if fresh:
                acc[slot, spot_of(slot, half), :] = value
            else:
                acc[slot, spot_of(slot, half), :] += value

    every = (-1, 0, 1)
    own_halo.wait()
    gather_sums(own, inner_half, 0, (every, every, every), True, True)
    next_early.wait_send()
    next_rest.start()
    gather_sums(own, outer_half, 0, (every, every, (0, 1)), True, True)

    next_early.wait_recv()
    next_halo.start()

    frame_total.wait()
    clip_end = clip_ref[later] == 1
    later_total = jnp.where(clip_end, total[...], total_in[...])
    pooled = jnp.concatenate(
        [
            (total[...] / (2.0 * cells)).astype(jnp.bfloat16),
            (later_total / (2.0 * cells)).astype(jnp.bfloat16),
        ],
        axis=1,
    )
    feature = jnp.maximum(dot_nt(pooled, pool_w[...]), 0.0).astype(jnp.bfloat16)
    width = point_w.shape[0]
    bias = dot_nt(feature, proj_w[:, pl.ds(4 * width, width)])[0:1]

    def choose(start, count):
        @pl.loop(0, count // 2)
        def _(k):
            spot = pl.ds(pl.multiple_of(start + k * 2 * cols, 16), 2 * cols)
            nxt[spot, :] = jnp.where(clip_end, own[spot, :], nxt[spot, :])

    next_halo.wait()
    choose(early_mine, EARLY)
    choose(pl.multiple_of((REACH + rows) * cols * (1 - r), 16), REACH)
    gather_sums(nxt, inner_half, 1, ((0, 1), (0, 1), (0, 1)), True, False)
    gather_sums(nxt, outer_half, 1, ((), (1,), (1,)), False, False)
    next_rest.wait()
    choose(rest_mine, rows - EARLY)

    edge_src = pl.multiple_of((HEAD_REACH + (rows - HEAD_REACH) * (1 - r)) * cols, 16)
    edge_dst = pl.multiple_of((HEAD_REACH + rows) * cols * r, 16)
    edge_copy = remote(
        6,
        projected.at[pl.ds(edge_src, edge)],
        projected.at[pl.ds(edge_dst, edge)],
        (g, t, sister),
    )

    def project(half, plan, with_point):
        sums = []
        for slot, value in enumerate(branch_sums(nxt, half, 1, plan, with_point)):
            full = acc[slot, spot_of(slot, half), :]
            sums.append(full if value is None else full + value)
        mixed = bias
        for b in range(4):
            if b == 0:
                full = sums[0]
            else:
                spread = DILATIONS[b - 1]
                full = (
                    sums[3 * b - 1]
                    + moved(sums[3 * b - 2], -spread)
                    + moved(sums[3 * b], spread)
                )
            branch = jnp.maximum(full, 0.0).astype(jnp.bfloat16)
            mixed = mixed + dot_nt(branch, proj_w[:, pl.ds(b * width, width)])
        spot = pl.ds(pl.multiple_of(HEAD_REACH * cols + half * tile, 16), tile)
        projected[spot, :] = jnp.maximum(mixed, 0.0).astype(jnp.bfloat16)

    project(inner_half, ((-1,), (-1,), (-1,)), False)
    edge_copy.start()
    project(outer_half, (every, (-1, 0), (0,)), True)

    size = 2 * HEAD_REACH + 1

    def head_tile(k):
        base = HEAD_REACH * cols + k * tile
        window = jnp.concatenate(
            [
                projected[pl.ds(pl.multiple_of(base + (i - HEAD_REACH) * cols, 16), tile), :]
                for i in range(size)
            ],
            axis=1,
        )
        value = None
        for j in range(size):
            taps = jnp.concatenate([head_w[size * i + j] for i in range(size)], axis=1)
            piece = dot_nt(window, taps)
            if j != HEAD_REACH:
                piece = moved(piece, j - HEAD_REACH)
            value = piece if value is None else value + piece
        head = jnp.maximum(value, 0.0).astype(jnp.bfloat16)
        weights = out_full[...].astype(jnp.bfloat16)
        maps = [
            dot_nt(weights, head[y * cols : (y + 1) * cols]) for y in range(tile_rows)
        ]
        for c in range(4):
            pred_ref[0, c, pl.ds(pl.multiple_of(k * tile_rows, 8), tile_rows), :] = (
                jnp.concatenate([value[c : c + 1] for value in maps], axis=0)
            )

    head_tile(outer_half)
    edge_copy.wait()
    head_tile(inner_half)

    gap = pred_ref[0, 0] - heat_map[...]
    offset_gap = jnp.abs(pred_ref[0, 1] - aim_map[0]) + jnp.abs(pred_ref[0, 2] - aim_map[1])
    err[...] = jnp.zeros(err.shape, jnp.float32)
    err[0:1, pl.ds(0, cols)] = jnp.sum(gap * gap, axis=0, keepdims=True)
    err[1:2, pl.ds(0, cols)] = jnp.sum(
        jnp.where(counted, offset_gap, 0.0), axis=0, keepdims=True
    )
    err[2:3, pl.ds(0, cols)] = jnp.sum(jnp.where(counted, 1.0, 0.0), axis=0, keepdims=True)
    err_all[mine] = err[...]

    def spread_copy(step, slot):
        return pltpu.make_async_remote_copy(
            src_ref=err,
            dst_ref=err_all.at[slot],
            send_sem=all_send_sem.at[step],
            recv_sem=all_recv_sem.at[slot],
            device_id=(g, slots[step] // 2, slots[step] % 2),
            device_id_type=MESH,
        )

    for step in range(bands - 1):
        spread_copy(step, mine).start()
    for step in range(bands - 1):
        spread_copy(step, mine).wait_send()
        spread_copy(step, slots[step]).wait_recv()
    summed = err_all[0]
    for slot in range(1, bands):
        summed = summed + err_all[slot]
    sums = jnp.sum(summed, axis=1, keepdims=True)
    center_loss = sums[0:1] / (frame_count * 2 * cells)
    offset_loss = offset_weight * sums[1:2] / jnp.maximum(sums[2:3], 1.0)
    losses_ref[0] = center_loss[0, 0]
    losses_ref[1] = offset_loss[0, 0]


def shards(
    frames,
    clip_start,
    semantic,
    instance,
    aspp_point,
    aspp_dilated,
    pool_weight,
    proj_weight,
    head_weight,
    out_weight,
):
    _, channels, rows, cols = frames.shape
    cells = rows * cols
    frame_count = clip_start.shape[0]
    width = aspp_point.shape[0]
    tile_rows = rows // 2
    place = np.zeros((8, cells), np.float32)
    place[0] = 1.0
    place[1] = np.arange(cells) // cols
    place[2] = np.arange(cells) % cols
    x = frames[0].reshape(channels, cells).T
    vmem = pl.BlockSpec(memory_space=pltpu.VMEM)
    anywhere = pl.BlockSpec(memory_space=pl.ANY)
    taps = aspp_dilated.shape[0] * aspp_dilated.shape[1]
    head_taps = head_weight.shape[0]
    tall = cells + 2 * REACH * cols
    bf16, f32 = jnp.bfloat16, jnp.float32
    return pl.pallas_call(
        functools.partial(kernel, frame_count, rows, cols, tile_rows),
        out_shape=(
            jax.ShapeDtypeStruct((1, 4, rows, cols), f32),
            jax.ShapeDtypeStruct((2,), f32),
        ),
        in_specs=[
            anywhere,
            pl.BlockSpec(memory_space=pltpu.SMEM),
            vmem,
            vmem,
            vmem,
            anywhere,
            anywhere,
            anywhere,
            anywhere,
            anywhere,
            vmem,
        ],
        out_specs=(vmem, pl.BlockSpec(memory_space=pltpu.SMEM)),
        scratch_shapes=[
            pltpu.VMEM((tall, channels), bf16),
            pltpu.VMEM((tall, channels), bf16),
            pltpu.VMEM((10, cells, width), f32),
            pltpu.VMEM(aspp_point.shape, bf16),
            pltpu.VMEM((taps,) + aspp_dilated.shape[2:], bf16),
            pltpu.VMEM(pool_weight.shape, bf16),
            pltpu.VMEM(proj_weight.shape, bf16),
            pltpu.VMEM((head_taps, LANES, width), bf16),
            pltpu.VMEM((cells + 2 * HEAD_REACH * cols, width), bf16),
            pltpu.VMEM((rows, cols), f32),
            pltpu.VMEM((2, rows, cols), f32),
            pltpu.VMEM((8, LANES), f32),
            pltpu.VMEM((8, LANES + channels), f32),
            pltpu.VMEM((8, LANES + channels), f32),
            pltpu.VMEM((8, channels), f32),
            pltpu.VMEM((8, channels), f32),
            pltpu.VMEM((8, LANES), f32),
            pltpu.VMEM((2 * frame_count, 8, LANES), f32),
            pltpu.SemaphoreType.DMA((6,)),
            pltpu.SemaphoreType.DMA((7,)),
            pltpu.SemaphoreType.DMA((7,)),
            pltpu.SemaphoreType.DMA((2 * frame_count - 1,)),
            pltpu.SemaphoreType.DMA((2 * frame_count,)),
        ],
        compiler_params=pltpu.CompilerParams(
            collective_id=0, has_side_effects=True, vmem_limit_bytes=56 * 1024 * 1024
        ),
    )(
        x,
        clip_start,
        semantic,
        instance,
        jnp.asarray(place),
        aspp_point,
        aspp_dilated.reshape((taps,) + aspp_dilated.shape[2:]),
        pool_weight,
        proj_weight,
        head_weight,
        out_weight,
    )


def solution(mesh):
    placed = (
        P(("grp", "tm"), None, "row", None),
        P("grp"),
        P(("grp", "tm"), "row", None),
        P(("grp", "tm"), "row", None),
        P(),
        P(),
        P(),
        P(),
        P(),
        P(),
    )
    return jax.shard_map(
        shards,
        mesh=mesh,
        in_specs=placed,
        out_specs=(P(("grp", "tm"), None, "row", None), P("grp")),
        check_vma=False,
    )
```
